32 devices in a mesh: ctx: 8 (over y, x, core), ch: 4 (over z).
Axes of the slice: x: 2, y: 2, z: 4, core: 2. Of those that a mesh axis runs over, the one named last changes fastest.
Arguments:
- gate_input: bfloat16 [8192, 4096], P('ch', 'ctx'), may hold values from -90 to 90
- key_input: bfloat16 [8192, 4096], P('ch', 'ctx'), may hold values from -6 to 6
- value_input: bfloat16 [8192, 4096], P('ch', 'ctx'), may hold values from -6 to 6
- short_filter: float32 [3, 3, 8192], P(None, None, 'ch'), may hold values from -3.5 to 3.5
- mr_filter: float32 [512, 128], P('ch'), may hold values from -0.5 to 0.5
- mr_skip: float32 [8192], P('ch'), may hold values from -3 to 3
- norm_gain: float32 [8192], P('ch'), may hold values from 0.5 to 1.5
- doc_lengths: int32 [16], replicated, may hold values from 1 to 2048, 4096 in all
Outputs:
- relaid: bfloat16 [8192, 4096], P(('ch', 'ctx'))
The draws below stay inside these ranges and needn't reach their ends.
Inputs may be any that keep to these rules, and one draw needn't show every extreme that they name: `doc_lengths`: the 16 lengths sum to 4096, and one of them is exactly 2048.
All inputs are finite; a program needn't handle non-finite values.
Results may differ from the reference program's by a relative error of at most 0.0095.
Values may be sent and summed in bfloat16 or wider, within the bound.
A program may use at most 128 MiB of HBM per device.

```python
import math
import jax
import jax.numpy as jnp
import numpy as np
from jax import lax

D = 8192
GROUP = 16
GROUPS = 512
SHORT = 3
MR = 128
TOKENS = 4096
DOCS = 16
DOC_MOST = 2048


def draw_gate_input(key, part):
    noise_key, chan_key, row_key = jax.random.split(key, 3)
    chan_place = jnp.arange(D, dtype=jnp.float32) / D
    chan_scale = jnp.exp(jax.random.uniform(chan_key, (D, 1), jnp.float32) * math.log(10.0)) * jnp.sqrt(1.0 + 2.0 * chan_place)[:, None]
    row_scale = jnp.exp(jax.random.uniform(row_key, (1, TOKENS), jnp.float32) * math.log(10.0))
    base_values = jnp.clip(jax.random.normal(noise_key, (D, TOKENS), jnp.float32), -5.0, 5.0)
    return (base_values * chan_scale * row_scale / 10.0).astype(jnp.bfloat16)


def steps_of(rng, dims, shards, low, largest):
    def one(axis_at, parts):
        heights = jax.random.uniform(jax.random.fold_in(jax.random.fold_in(rng, 6), axis_at), (parts,), jnp.float32, low / len(shards), largest / len(shards))
        return jnp.repeat(jnp.exp(heights), dims[axis_at] // parts).reshape((-1,) + (1,) * (len(dims) - axis_at - 1))

    factor_of = one(*shards[0])
    for cut in shards[1:]:
        factor_of = factor_of * one(*cut)
    return factor_of


def length_profile(number_of, total, limit, slope):
    weights = [(1 << 20) // math.isqrt(standing ** slope) + 1 for standing in range(2, number_of + 1)]
    rest, counts = total - limit - (number_of - 1), [1] * (number_of - 1)
    while rest > 0:
        candidates = [i for i in range(number_of - 1) if counts[i] < limit]
        pool, left = sum([weights[i] for i in candidates]), rest
        for i in candidates:
            addition = min(limit - counts[i], max(1, left * weights[i] // pool), rest)
            counts[i] = counts[i] + addition
            rest = rest - addition
    return np.array([limit] + counts)


def ragged_sizes(key, amount, total, reach, skew):
    if amount == 2:
        one = jax.random.randint(key, (), max(1, total - reach), min(reach, total - 1) + 1)
        return jnp.stack([one, total - one])
    tallies = jnp.asarray(length_profile(amount, total, reach, skew), jnp.int32)
    twos = (amount - 1) // 2
    donor, receiver = tallies[1:1 + 2 * twos:2], tallies[2:2 + 2 * twos:2]
    margin = jnp.minimum(donor - 1, reach - receiver)
    moved = jax.random.randint(jax.random.fold_in(key, 1), (twos,), 0, 1 << 20) % (margin + 1)
    tallies = tallies.at[1:1 + 2 * twos:2].set(donor - moved).at[2:2 + 2 * twos:2].set(receiver + moved)
    return tallies[jax.random.permutation(jax.random.fold_in(key, 2), amount)]


def bell_draw(own_key, dims, width, most, shards=(), held_as=jnp.bfloat16):
    loudness = steps_of(own_key, dims, shards, -0.22, 0.18) if shards else 1.0
    drawn = jax.random.normal(own_key, dims, jnp.float32) * width * loudness
    return jnp.minimum(jnp.maximum(drawn, -most), most).astype(held_as)


def setup_inputs(seed: int = 0) -> dict:
    keys = jax.random.split(jax.random.key(seed), 9)
    gate_input = draw_gate_input(jax.random.fold_in(keys[8], 71), 0)
    key_input = bell_draw(keys[1], (D, TOKENS), 1.0, 6.0, ((0, 4), (1, 8)))
    value_input = bell_draw(keys[2], (D, TOKENS), 1.0, 6.0, ((0, 4), (1, 8)))
    short_filter = bell_draw(keys[3], (3, SHORT, D), SHORT ** -0.5, 3.5, ((2, 4),), jnp.float32)
    mr_filter = bell_draw(keys[4], (GROUPS, MR), MR ** -0.5, 0.5, ((0, 4),), jnp.float32)
    mr_skip = bell_draw(keys[5], (D,), 1.0, 3.0, ((0, 4),), jnp.float32)
    norm_gain = jnp.clip(1.0 + 0.1 * jax.random.normal(keys[6], (D,), jnp.float32), 0.5, 1.5)
    doc_lengths = ragged_sizes(keys[7], DOCS, TOKENS, DOC_MOST, 2).astype(jnp.int32)
    return dict(gate_input=gate_input, key_input=key_input, value_input=value_input, short_filter=short_filter, mr_filter=mr_filter, mr_skip=mr_skip, norm_gain=norm_gain, doc_lengths=doc_lengths)


NORM_EPS = 1e-06

def doc_starts(doc_lengths, positions):
    doc_ends = jnp.cumsum(doc_lengths).astype(jnp.int32)
    doc_firsts = (doc_ends - doc_lengths).astype(jnp.int32)
    before_row = doc_firsts[:, None] <= positions[None, :]
    return lax.optimization_barrier(jnp.max(jnp.where(before_row, doc_firsts[:, None], 0), axis=0)).astype(jnp.int32)

def short_conv(raw_rows, prior_rows, tap_rows, positions, starts):
    row_count = raw_rows.shape[1]
    extended = jnp.concatenate([prior_rows, raw_rows], axis=1).astype(jnp.float32)
    running = jnp.zeros(raw_rows.shape, jnp.float32)
    for tap_lag in range(SHORT):
        lagged = lax.slice_in_dim(extended, SHORT - 1 - tap_lag, SHORT - 1 - tap_lag + row_count, axis=1)
        in_document = positions - tap_lag >= starts
        running = running + jnp.where(in_document[None, :], tap_rows[tap_lag][:, None] * lagged, 0.0)
    return running

def toeplitz(taps_bf):
    row_index = np.arange(2 * MR)[:, None]
    col_index = np.arange(MR)[None, :]
    tap_lag = col_index + MR - row_index
    is_valid = (tap_lag >= 0) & (tap_lag < MR)
    index_table = np.clip(tap_lag, 0, MR - 1)
    return jnp.where(is_valid[None], taps_bf[:, index_table], jnp.zeros((), jnp.bfloat16))

def long_conv(values, prior_rows, taps_bf, first_row, starts):
    channels, row_count = values.shape
    groups = taps_bf.shape[0]
    members = channels // groups
    tile_count = row_count // MR
    blocked = jnp.concatenate([prior_rows, values], axis=1).reshape(channels, tile_count + 1, MR)
    windows = jnp.concatenate([blocked[:, :-1], blocked[:, 1:]], axis=2).reshape(groups, members, tile_count, 2 * MR)
    matrices = toeplitz(taps_bf)
    per_step = math.gcd(tile_count, max(1, 64 // groups))
    tile_starts = starts.reshape(tile_count, MR)
    source_offsets = jnp.arange(2 * MR, dtype=jnp.int32) - MR
    step_offsets = jnp.arange(per_step, dtype=jnp.int32) * MR
    zero_bf = jnp.zeros((), jnp.bfloat16)

    def advance(step_index, result):
        block_begin = step_index * per_step
        window_part = lax.dynamic_slice_in_dim(windows, block_begin, per_step, axis=2)
        row_starts = lax.dynamic_slice_in_dim(tile_starts, block_begin, per_step, axis=0)
        tile_first = first_row + block_begin * MR + step_offsets
        sources = tile_first[:, None] + source_offsets[None, :]
        allowed = sources[:, :, None] >= row_starts[:, None, :]
        masked = jnp.where(allowed[:, None], matrices[None], zero_bf)
        product = jnp.einsum('gcns,ngst->gcnt', window_part.astype(jnp.float32), masked.astype(jnp.float32))
        return lax.dynamic_update_slice_in_dim(result, product, block_begin, axis=2)
    result = lax.fori_loop(0, tile_count // per_step, advance, jnp.zeros((groups, members, tile_count, MR), jnp.float32))
    return result.reshape(channels, row_count)

def reference(gate_input, key_input, value_input, short_filter, mr_filter, mr_skip, norm_gain, doc_lengths):
    positions = jnp.arange(TOKENS, dtype=jnp.int32)
    starts = doc_starts(doc_lengths, positions)
    chan_block = min(D, 1024)
    zero_prior = jnp.zeros((chan_block, SHORT - 1), jnp.bfloat16)
    zero_rows = jnp.zeros((chan_block, MR), jnp.bfloat16)
    squares = jnp.zeros((TOKENS,), jnp.float32)
    pieces = []
    for block_index in range(D // chan_block):
        chan_first = block_index * chan_block
        chan_last = chan_first + chan_block
        gate_conv = short_conv(gate_input[chan_first:chan_last], zero_prior, short_filter[0, :, chan_first:chan_last], positions, starts)
        key_conv = short_conv(key_input[chan_first:chan_last], zero_prior, short_filter[1, :, chan_first:chan_last], positions, starts)
        value_conv = short_conv(value_input[chan_first:chan_last], zero_prior, short_filter[2, :, chan_first:chan_last], positions, starts)
        product_rows = (key_conv * value_conv).astype(jnp.bfloat16)
        taps_bf = mr_filter[chan_first // GROUP:chan_last // GROUP].astype(jnp.bfloat16)
        mixed_rows = long_conv(product_rows, zero_rows, taps_bf, 0, starts) + mr_skip[chan_first:chan_last, None] * product_rows.astype(jnp.float32)
        gated = gate_conv * mixed_rows
        squares = squares + lax.optimization_barrier(jnp.sum(gated * gated, axis=0))
        pieces.append(gated)
    row_scale = lax.rsqrt(squares / D + NORM_EPS)
    results = []
    for block_index in range(D // chan_block):
        chan_first = block_index * chan_block
        gain_part = norm_gain[chan_first:chan_first + chan_block]
        results.append((pieces[block_index] * row_scale[None, :] * gain_part[:, None]).astype(jnp.bfloat16))
    return jnp.concatenate(results, axis=0)
```

```python
import functools

import jax
import jax.numpy as jnp
from jax import lax
from jax.experimental import pallas as pl
from jax.experimental.pallas import tpu as pltpu
from jax.sharding import PartitionSpec as P

D = 8192
GROUP = 16
SHORT = 3
MR = 128
NORM_EPS = 1e-06

LANES = 128
BLOCK = 256
F32 = jnp.float32
BF16 = jnp.bfloat16


def short_conv(ext_ref, coef_ref, rows, first_tile, tiles, which, m1, m2):
    width = (tiles + 1) * LANES
    x = ext_ref[rows, first_tile * LANES : first_tile * LANES + width].astype(F32)
    x1 = pltpu.roll(x, 1, 1)[:, LANES:]
    x2 = pltpu.roll(x, 2, 1)[:, LANES:]
    base = which * SHORT
    c0 = coef_ref[rows, base : base + 1]
    c1 = coef_ref[rows, base + 1 : base + 2]
    c2 = coef_ref[rows, base + 2 : base + 3]
    return c0 * x[:, LANES:] + c1 * (x1 * m1) + c2 * (x2 * m2)


def kernel(
    n,
    nz,
    gate_hbm,
    key_hbm,
    value_hbm,
    sf_ref,
    mr_ref,
    skip_ref,
    docs_ref,
    recv_ref,
    scale_ref,
    g_ext,
    k_ext,
    v_ext,
    p_ext,
    circ,
    coef,
    masks,
    lagmask,
    sendbuf,
    raw_send,
    raw_recv,
    acc,
    sq_all,
    sc_all,
    load_sem,
    halo_send,
    halo_recv,
    data_send,
    data_recv,
    sq_send,
    sq_recv,
    sc_send,
    sc_recv,
):
    me = lax.axis_index("ctx")
    mz = lax.axis_index("ch")
    channels, rows_here = gate_hbm.shape
    chunk = channels // n
    groups = channels // GROUP
    tiles = rows_here // LANES
    blocks = channels // BLOCK
    barrier = pltpu.get_barrier_semaphore()

    def load(b, which):
        source = (gate_hbm, key_hbm, value_hbm)[which]
        target = (g_ext, k_ext, v_ext)[which]
        span = pl.ds(pl.multiple_of(b * BLOCK, BLOCK), BLOCK)
        return pltpu.make_async_copy(
            source.at[span, :],
            target.at[span, LANES : LANES + rows_here],
            load_sem.at[b, which],
        )

    for b in range(blocks):
        for which in range(3):
            load(b, which).start()
    for k in range(1, n):
        pl.semaphore_signal(barrier, inc=1, device_id={"ctx": lax.rem(me + k, n)})
    for k in range(1, nz):
        pl.semaphore_signal(barrier, inc=1, device_id={"ch": lax.rem(mz + k, nz)})

    positions = me * rows_here + lax.broadcasted_iota(jnp.int32, (1, rows_here), 1)
    starts = jnp.zeros((1, rows_here), jnp.int32)
    first = jnp.int32(0)
    for d in range(docs_ref.shape[0]):
        starts = jnp.where(positions >= first, first, starts)
        first = first + docs_ref[d]
    for lag in (1, 2):
        lagmask[lag : lag + 1, :] = jnp.where(positions - lag >= starts, 1.0, 0.0).astype(F32)
    s_index = lax.broadcasted_iota(jnp.int32, (LANES, LANES), 0)
    t_index = lax.broadcasted_iota(jnp.int32, (LANES, LANES), 1)
    for tile in range(tiles):
        start_row = starts[:, tile * LANES : (tile + 1) * LANES]
        here = me * rows_here + tile * LANES + s_index
        before = (t_index < s_index) & (here - LANES >= start_row)
        within = (t_index >= s_index) & (here >= start_row)
        masks[tile, 0:LANES, :] = jnp.where(before, 1.0, 0.0).astype(BF16)
        masks[tile, LANES : 2 * LANES, :] = jnp.where(within, 1.0, 0.0).astype(BF16)

    for b in range(channels // LANES):
        span = slice(b * LANES, (b + 1) * LANES)
        parts = [sf_ref[a, :, span] for a in range(3)] + [skip_ref[:, span]]
        parts.append(jnp.zeros((LANES - 10, LANES), F32))
        coef[span, :] = jnp.concatenate(parts, axis=0).T

    row16 = lax.broadcasted_iota(jnp.int32, (16, LANES), 0)
    lane16 = lax.broadcasted_iota(jnp.int32, (16, LANES), 1)

    def pick(which):
        hit = (lane16 - (LANES - 2) == row16 - 2 * which) & (lane16 >= LANES - 2)
        return jnp.where(hit, 1.0, 0.0).astype(BF16)

    last = tiles * LANES

    def halo_block(b, carry):
        for which in range(3):
            load(b, which).wait()
        span = pl.ds(pl.multiple_of(b * BLOCK, BLOCK), BLOCK)
        columns = jnp.zeros((16, BLOCK), F32)
        for which, ref in enumerate((g_ext, k_ext, v_ext)):
            columns = columns + lax.dot_general(
                pick(which),
                ref[span, last : last + LANES],
                (((1,), (1,)), ((), ())),
                preferred_element_type=F32,
            )
        raw_send[:, span] = columns.astype(BF16)
        m1 = lagmask[1:2, last - LANES : last]
        m2 = lagmask[2:3, last - LANES : last]

        def halo_rows(i, c):
            rows = pl.ds(pl.multiple_of(b * BLOCK + i * 32, 32), 32)
            kc = short_conv(k_ext, coef, rows, tiles - 1, 1, 1, m1, m2)
            vc = short_conv(v_ext, coef, rows, tiles - 1, 1, 2, m1, m2)
            p_ext[rows, last : last + LANES] = (kc * vc).astype(BF16)
            return c

        lax.fori_loop(0, BLOCK // 32, halo_rows, 0, unroll=2)
        return carry

    lax.fori_loop(0, blocks, halo_block, 0)

    pl.semaphore_wait(barrier, n - 1 + nz - 1)
    right = lax.rem(me + 1, n)

    def raw_copy():
        return pltpu.make_async_remote_copy(
            src_ref=raw_send,
            dst_ref=raw_recv,
            send_sem=halo_send.at[0],
            recv_sem=halo_recv.at[0],
            device_id={"ctx": right},
        )

    def product_copy():
        return pltpu.make_async_remote_copy(
            src_ref=p_ext.at[:, last : last + LANES],
            dst_ref=p_ext.at[:, 0:LANES],
            send_sem=halo_send.at[1],
            recv_sem=halo_recv.at[1],
            device_id={"ctx": right},
        )

    @pl.when(me < n - 1)
    def _():
        raw_copy().start()
        product_copy().start()

    @pl.when(me == 0)
    def _():
        raw_recv[...] = jnp.zeros(raw_recv.shape, BF16)
        p_ext[:, 0:LANES] = jnp.zeros((channels, LANES), BF16)

    def build(g, carry):
        taps = jnp.broadcast_to(mr_ref[pl.ds(g, 1), :], (LANES, LANES))
        turned = pltpu.roll(taps, 0, 1, stride=1, stride_axis=0)
        circ[g] = turned.astype(BF16)
        return carry

    lax.fori_loop(0, groups, build, 0, unroll=2)

    @pl.when(me > 0)
    def _():
        raw_copy().wait_recv()

    def spread(b, carry):
        span = pl.ds(pl.multiple_of(b * BLOCK, BLOCK), BLOCK)
        for which, ref in enumerate((g_ext, k_ext, v_ext)):
            ref[span, 0:LANES] = lax.dot_general(
                raw_recv[:, span],
                pick(which),
                (((0,), (0,)), ((), ())),
                preferred_element_type=F32,
            ).astype(BF16)
        return carry

    lax.fori_loop(0, blocks, spread, 0)

    def products(i, carry):
        rows = pl.ds(pl.multiple_of(i * GROUP, GROUP), GROUP)
        m1 = lagmask[1:2, 0 : last - LANES]
        m2 = lagmask[2:3, 0 : last - LANES]
        kc = short_conv(k_ext, coef, rows, 0, tiles - 1, 1, m1, m2)
        vc = short_conv(v_ext, coef, rows, 0, tiles - 1, 2, m1, m2)
        p_ext[rows, LANES:last] = (kc * vc).astype(BF16)
        return carry

    lax.fori_loop(0, groups, products, 0, unroll=2)

    acc[...] = jnp.zeros(acc.shape, F32)

    def mix(g, first_tile, count):
        rows = pl.ds(pl.multiple_of(g * GROUP, GROUP), GROUP)
        lanes = slice(first_tile * LANES, (first_tile + count) * LANES)
        c = circ[g]
        pair = jnp.concatenate([c, c], axis=0)
        parts = []
        for tile in range(first_tile, first_tile + count):
            parts.append(
                jnp.dot(
                    p_ext[rows, tile * LANES : (tile + 2) * LANES],
                    pair * masks[tile],
                    preferred_element_type=F32,
                )
            )
        mixed = parts[0] if count == 1 else jnp.concatenate(parts, axis=1)
        direct = p_ext[rows, (first_tile + 1) * LANES : (first_tile + 1 + count) * LANES]
        mixed = mixed + coef[rows, 9:10] * direct.astype(F32)
        gate = short_conv(
            g_ext, coef, rows, first_tile, count, 0, lagmask[1:2, lanes], lagmask[2:3, lanes]
        )
        gated = gate * mixed
        sendbuf[rows, lanes] = gated.astype(BF16)
        squares = gated * gated
        return squares[0:8] + squares[8:16]

    def data_copy(dest, source, half):
        lanes = (LANES, last - LANES) if half == 0 else (0, LANES)
        return pltpu.make_async_remote_copy(
            src_ref=sendbuf.at[
                pl.ds(pl.multiple_of(dest * chunk, chunk), chunk), lanes[0] : lanes[0] + lanes[1]
            ],
            dst_ref=recv_ref.at[
                :, pl.ds(pl.multiple_of(source * rows_here + lanes[0], LANES), lanes[1])
            ],
            send_sem=data_send.at[dest, half],
            recv_sem=data_recv.at[source, half],
            device_id={"ctx": dest},
        )

    def own_copy(half):
        lanes = (LANES, last - LANES) if half == 0 else (0, LANES)
        return pltpu.make_async_copy(
            sendbuf.at[
                pl.ds(pl.multiple_of(me * chunk, chunk), chunk), lanes[0] : lanes[0] + lanes[1]
            ],
            recv_ref.at[:, pl.ds(pl.multiple_of(me * rows_here + lanes[0], LANES), lanes[1])],
            data_send.at[me, half],
        )

    def stage(half, first_tile, count, together):
        lanes = slice(first_tile * LANES, (first_tile + count) * LANES)
        chunk_groups = chunk // GROUP

        def one(step, carry):
            k = lax.rem(step + 2, n)
            dest = lax.rem(me + k, n)

            def some(i, c):
                total = jnp.zeros((8, count * LANES), F32)
                for j in range(together):
                    total = total + mix(
                        dest * chunk_groups + i * together + j, first_tile, count
                    )
                acc[:, lanes] += total
                return c

            lax.fori_loop(0, chunk_groups // together, some, 0)

            @pl.when(k != 0)
            def _():
                data_copy(dest, me, half).start()

            @pl.when(k == 0)
            def _():
                own_copy(half).start()

            return carry

        lax.fori_loop(0, n, one, 0)

    stage(0, 1, tiles - 1, 2)

    @pl.when(me > 0)
    def _():
        product_copy().wait_recv()

    stage(1, 0, 1, 2)

    sq_all[mz] = jnp.sum(acc[...], axis=0, keepdims=True)

    def sq_copy(dest, source):
        return pltpu.make_async_remote_copy(
            src_ref=sq_all.at[mz],
            dst_ref=sq_all.at[source],
            send_sem=sq_send.at[dest],
            recv_sem=sq_recv.at[source],
            device_id={"ch": dest},
        )

    for k in range(1, nz):
        sq_copy(lax.rem(mz + k, nz), mz).start()
    for k in range(1, nz):
        sq_copy(mz, lax.rem(mz + k, nz)).wait_recv()
    total = sq_all[0]
    for z in range(1, nz):
        total = total + sq_all[z]
    sc_all[me] = lax.rsqrt(total / D + NORM_EPS)

    def sc_copy(dest, source):
        return pltpu.make_async_remote_copy(
            src_ref=sc_all.at[me],
            dst_ref=sc_all.at[source],
            send_sem=sc_send.at[dest],
            recv_sem=sc_recv.at[source],
            device_id={"ctx": dest},
        )

    for k in range(1, n):
        sc_copy(lax.rem(me + k, n), me).start()
    for k in range(1, n):
        sc_copy(me, lax.rem(me + k, n)).wait_recv()
    scale_ref[...] = sc_all[...]

    def finish(k, carry):
        other = lax.rem(me + k, n)
        for half in (0, 1):
            data_copy(me, other, half).wait_recv()
            data_copy(other, me, half).wait_send()
        sc_copy(other, me).wait_send()
        return carry

    lax.fori_loop(1, n, finish, 0)
    own_copy(0).wait()
    own_copy(1).wait()
    for k in range(1, nz):
        sq_copy(lax.rem(mz + k, nz), mz).wait_send()

    @pl.when(me < n - 1)
    def _():
        raw_copy().wait_send()
        product_copy().wait_send()


def local(
    n, nz, gate_input, key_input, value_input, short_filter, mr_filter, mr_skip, norm_gain, doc_lengths
):
    channels, rows_here = gate_input.shape
    chunk = channels // n
    groups = channels // GROUP
    tiles = rows_here // LANES
    ext = pltpu.VMEM((channels, rows_here + LANES), BF16)
    anywhere = pl.BlockSpec(memory_space=pl.ANY)
    vmem = pl.BlockSpec(memory_space=pltpu.VMEM)
    dma = pltpu.SemaphoreType.DMA
    received, scales = pl.pallas_call(
        functools.partial(kernel, n, nz),
        out_shape=(
            jax.ShapeDtypeStruct((chunk, n * rows_here), BF16),
            jax.ShapeDtypeStruct((n, 1, rows_here), F32),
        ),
        in_specs=[
            anywhere,
            anywhere,
            anywhere,
            vmem,
            vmem,
            vmem,
            pl.BlockSpec(memory_space=pltpu.SMEM),
        ],
        out_specs=(anywhere, vmem),
        scratch_shapes=[
            ext,
            ext,
            ext,
            ext,
            pltpu.VMEM((groups, LANES, LANES), BF16),
            pltpu.VMEM((channels, LANES), F32),
            pltpu.VMEM((tiles, 2 * LANES, LANES), BF16),
            pltpu.VMEM((8, rows_here), F32),
            pltpu.VMEM((channels, rows_here), BF16),
            pltpu.VMEM((16, channels), BF16),
            pltpu.VMEM((16, channels), BF16),
            pltpu.VMEM((8, rows_here), F32),
            pltpu.VMEM((nz, 1, rows_here), F32),
            pltpu.VMEM((n, 1, rows_here), F32),
            dma((channels // BLOCK, 3)),
            dma((2,)),
            dma((2,)),
            dma((n, 2)),
            dma((n, 2)),
            dma((nz,)),
            dma((nz,)),
            dma((n,)),
            dma((n,)),
        ],
        compiler_params=pltpu.CompilerParams(
            collective_id=0, has_side_effects=True, vmem_limit_bytes=40 * 1024 * 1024
        ),
        cost_estimate=pl.CostEstimate(
            flops=channels * rows_here * 600, bytes_accessed=channels * rows_here * 8, transcendentals=0
        ),
    )(
        gate_input,
        key_input,
        value_input,
        short_filter,
        mr_filter,
        mr_skip.reshape(1, channels),
        doc_lengths,
    )
    gain_here = lax.dynamic_slice_in_dim(norm_gain, lax.axis_index("ctx") * chunk, chunk)
    row_scale = scales.reshape(1, n * rows_here)
    return (received.astype(F32) * row_scale * gain_here[:, None]).astype(BF16)


def solution(mesh):
    n, nz = mesh.shape["ctx"], mesh.shape["ch"]
    in_specs = (
        P("ch", "ctx"),
        P("ch", "ctx"),
        P("ch", "ctx"),
        P(None, None, "ch"),
        P("ch", None),
        P("ch"),
        P("ch"),
        P(),
    )
    out_specs = P(("ch", "ctx"), None)
    return jax.shard_map(
        functools.partial(local, n, nz), mesh=mesh, in_specs=in_specs, out_specs=out_specs, check_vma=False
    )
```

```python
import functools

import jax
import jax.numpy as jnp
from jax import lax
from jax.experimental import pallas as pl
from jax.experimental.pallas import tpu as pltpu
from jax.sharding import PartitionSpec as P

D = 8192
GROUP = 16
SHORT = 3
MR = 128
NORM_EPS = 1e-06

LANES = 128
BLOCK = 256
F32 = jnp.float32
BF16 = jnp.bfloat16


def short_conv(ext_ref, coef_ref, rows, first_tile, tiles, which, m1, m2):
    width = (tiles + 1) * LANES
    x = ext_ref[rows, first_tile * LANES : first_tile * LANES + width].astype(F32)
    x1 = pltpu.roll(x, 1, 1)[:, LANES:]
    x2 = pltpu.roll(x, 2, 1)[:, LANES:]
    base = which * SHORT
    c0 = coef_ref[rows, base : base + 1]
    c1 = coef_ref[rows, base + 1 : base + 2]
    c2 = coef_ref[rows, base + 2 : base + 3]
    return c0 * x[:, LANES:] + c1 * (x1 * m1) + c2 * (x2 * m2)


def kernel(
    n,
    nz,
    gate_hbm,
    key_hbm,
    value_hbm,
    sf_hbm,
    mr_hbm,
    skip_hbm,
    docs_ref,
    recv_ref,
    scale_ref,
    g_ext,
    k_ext,
    v_ext,
    p_ext,
    circ,
    coef,
    masks,
    lagmask,
    sendbuf,
    raw_send,
    raw_recv,
    acc,
    sq_all,
    sc_all,
    sf_ref,
    mr_ref,
    skip_ref,
    small_sem,
    load_sem,
    halo_send,
    halo_recv,
    data_send,
    data_recv,
    sq_send,
    sq_recv,
    sc_send,
    sc_recv,
):
    me = lax.axis_index("ctx")
    mz = lax.axis_index("ch")
    channels, rows_here = gate_hbm.shape
    chunk = channels // n
    groups = channels // GROUP
    tiles = rows_here // LANES
    blocks = channels // BLOCK
    barrier = pltpu.get_barrier_semaphore()

    def load(b, which):
        source = (gate_hbm, key_hbm, value_hbm)[which]
        target = (g_ext, k_ext, v_ext)[which]
        span = pl.ds(pl.multiple_of(b * BLOCK, BLOCK), BLOCK)
        return pltpu.make_async_copy(
            source.at[span, :],
            target.at[span, LANES : LANES + rows_here],
            load_sem.at[b, which],
        )

    small = [
        pltpu.make_async_copy(source, target, small_sem.at[i])
        for i, (source, target) in enumerate(
            ((sf_hbm, sf_ref), (skip_hbm, skip_ref), (mr_hbm, mr_ref))
        )
    ]
    for copy in small:
        copy.start()
    for b in range(blocks):
        for which in range(3):
            load(b, which).start()
    for k in range(1, n):
        pl.semaphore_signal(barrier, inc=1, device_id={"ctx": lax.rem(me + k, n)})
    for k in range(1, nz):
        pl.semaphore_signal(barrier, inc=1, device_id={"ch": lax.rem(mz + k, nz)})

    positions = me * rows_here + lax.broadcasted_iota(jnp.int32, (1, rows_here), 1)
    starts = jnp.zeros((1, rows_here), jnp.int32)
    first = jnp.int32(0)
    for d in range(docs_ref.shape[0]):
        starts = jnp.where(positions >= first, first, starts)
        first = first + docs_ref[d]
    for lag in (1, 2):
        lagmask[lag : lag + 1, :] = jnp.where(positions - lag >= starts, 1.0, 0.0).astype(F32)
    s_index = lax.broadcasted_iota(jnp.int32, (LANES, LANES), 0)
    t_index = lax.broadcasted_iota(jnp.int32, (LANES, LANES), 1)
    for tile in range(tiles):
        start_row = starts[:, tile * LANES : (tile + 1) * LANES]
        here = me * rows_here + tile * LANES + s_index
        before = (t_index < s_index) & (here - LANES >= start_row)
        within = (t_index >= s_index) & (here >= start_row)
        masks[tile, 0:LANES, :] = jnp.where(before, 1.0, 0.0).astype(BF16)
        masks[tile, LANES : 2 * LANES, :] = jnp.where(within, 1.0, 0.0).astype(BF16)

    for copy in small:
        copy.wait()

    for b in range(channels // LANES):
        span = slice(b * LANES, (b + 1) * LANES)
        parts = [sf_ref[a, :, span] for a in range(3)] + [skip_ref[:, span]]
        parts.append(jnp.zeros((6, LANES), F32))
        coef[span, 0:16] = jnp.concatenate(parts, axis=0).T

    row16 = lax.broadcasted_iota(jnp.int32, (16, LANES), 0)
    lane16 = lax.broadcasted_iota(jnp.int32, (16, LANES), 1)

    def pick(which):
        hit = (lane16 - (LANES - 2) == row16 - 2 * which) & (lane16 >= LANES - 2)
        return jnp.where(hit, 1.0, 0.0).astype(BF16)

    last = tiles * LANES

    def halo_block(b, carry):
        for which in range(3):
            load(b, which).wait()
        span = pl.ds(pl.multiple_of(b * BLOCK, BLOCK), BLOCK)
        columns = jnp.zeros((16, BLOCK), F32)
        for which, ref in enumerate((g_ext, k_ext, v_ext)):
            columns = columns + lax.dot_general(
                pick(which),
                ref[span, last : last + LANES],
                (((1,), (1,)), ((), ())),
                preferred_element_type=F32,
            )
        raw_send[:, span] = columns.astype(BF16)
        m1 = lagmask[1:2, last - LANES : last]
        m2 = lagmask[2:3, last - LANES : last]

        def halo_rows(i, c):
            rows = pl.ds(pl.multiple_of(b * BLOCK + i * 32, 32), 32)
            kc = short_conv(k_ext, coef, rows, tiles - 1, 1, 1, m1, m2)
            vc = short_conv(v_ext, coef, rows, tiles - 1, 1, 2, m1, m2)
            p_ext[rows, last : last + LANES] = (kc * vc).astype(BF16)
            return c

        lax.fori_loop(0, BLOCK // 32, halo_rows, 0, unroll=4)
        return carry

    lax.fori_loop(0, blocks, halo_block, 0)

    pl.semaphore_wait(barrier, n - 1 + nz - 1)
    right = lax.rem(me + 1, n)

    def raw_copy():
        return pltpu.make_async_remote_copy(
            src_ref=raw_send,
            dst_ref=raw_recv,
            send_sem=halo_send.at[0],
            recv_sem=halo_recv.at[0],
            device_id={"ctx": right},
        )

    def product_copy():
        return pltpu.make_async_remote_copy(
            src_ref=p_ext.at[:, last : last + LANES],
            dst_ref=p_ext.at[:, 0:LANES],
            send_sem=halo_send.at[1],
            recv_sem=halo_recv.at[1],
            device_id={"ctx": right},
        )

    @pl.when(me < n - 1)
    def _():
        raw_copy().start()
        product_copy().start()

    @pl.when(me == 0)
    def _():
        raw_recv[...] = jnp.zeros(raw_recv.shape, BF16)
        p_ext[:, 0:LANES] = jnp.zeros((channels, LANES), BF16)

    def build(g, carry):
        taps = jnp.broadcast_to(mr_ref[pl.ds(g, 1), :], (LANES, LANES))
        turned = pltpu.roll(taps, 0, 1, stride=1, stride_axis=0)
        circ[g] = turned.astype(BF16)
        return carry

    @pl.when(me > 0)
    def _():
        raw_copy().wait_recv()

    def spread(b, carry):
        span = pl.ds(pl.multiple_of(b * BLOCK, BLOCK), BLOCK)
        for which, ref in enumerate((g_ext, k_ext, v_ext)):
            ref[span, 0:LANES] = lax.dot_general(
                raw_recv[:, span],
                pick(which),
                (((0,), (0,)), ((), ())),
                preferred_element_type=F32,
            ).astype(BF16)
        return carry

    lax.fori_loop(0, blocks, spread, 0)

    def products(i, carry):
        rows = pl.ds(pl.multiple_of(i * GROUP, GROUP), GROUP)
        m1 = lagmask[1:2, 0 : last - LANES]
        m2 = lagmask[2:3, 0 : last - LANES]
        kc = short_conv(k_ext, coef, rows, 0, tiles - 1, 1, m1, m2)
        vc = short_conv(v_ext, coef, rows, 0, tiles - 1, 2, m1, m2)
        p_ext[rows, LANES:last] = (kc * vc).astype(BF16)
        return carry

    acc[...] = jnp.zeros(acc.shape, F32)

    def mix(g, first_tile, count):
        rows = pl.ds(pl.multiple_of(g * GROUP, GROUP), GROUP)
        lanes = slice(first_tile * LANES, (first_tile + count) * LANES)
        c = circ[g]
        pair = jnp.concatenate([c, c], axis=0)
        parts = []
        for tile in range(first_tile, first_tile + count):
            parts.append(
                jnp.dot(
                    p_ext[rows, tile * LANES : (tile + 2) * LANES],
                    pair * masks[tile],
                    preferred_element_type=F32,
                )
            )
        mixed = parts[0] if count == 1 else jnp.concatenate(parts, axis=1)
        direct = p_ext[rows, (first_tile + 1) * LANES : (first_tile + 1 + count) * LANES]
        mixed = mixed + coef[rows, 9:10] * direct.astype(F32)
        gate = short_conv(
            g_ext, coef, rows, first_tile, count, 0, lagmask[1:2, lanes], lagmask[2:3, lanes]
        )
        gated = gate * mixed
        sendbuf[rows, lanes] = gated.astype(BF16)
        squares = gated * gated
        return squares[0:8] + squares[8:16]

    def data_copy(dest, source, half):
        lanes = (LANES, last - LANES) if half == 0 else (0, LANES)
        return pltpu.make_async_remote_copy(
            src_ref=sendbuf.at[
                pl.ds(pl.multiple_of(dest * chunk, chunk), chunk), lanes[0] : lanes[0] + lanes[1]
            ],
            dst_ref=recv_ref.at[
                :, pl.ds(pl.multiple_of(source * rows_here + lanes[0], LANES), lanes[1])
            ],
            send_sem=data_send.at[dest, half],
            recv_sem=data_recv.at[source, half],
            device_id={"ctx": dest},
        )

    def own_copy(half):
        lanes = (LANES, last - LANES) if half == 0 else (0, LANES)
        return pltpu.make_async_copy(
            sendbuf.at[
                pl.ds(pl.multiple_of(me * chunk, chunk), chunk), lanes[0] : lanes[0] + lanes[1]
            ],
            recv_ref.at[:, pl.ds(pl.multiple_of(me * rows_here + lanes[0], LANES), lanes[1])],
            data_send.at[me, half],
        )

    def stage(half, first_tile, count, together):
        lanes = slice(first_tile * LANES, (first_tile + count) * LANES)
        chunk_groups = chunk // GROUP

        def one(step, carry):
            k = lax.rem(step + 2, n)
            dest = lax.rem(me + k, n)

            if half == 0:
                first = dest * chunk_groups
                unroll = min(4, chunk_groups)
                lax.fori_loop(
                    0, chunk_groups, lambda i, c: build(first + i, c), 0, unroll=unroll
                )
                lax.fori_loop(
                    0, chunk_groups, lambda i, c: products(first + i, c), 0, unroll=unroll
                )

            def some(i, c):
                total = jnp.zeros((8, count * LANES), F32)
                for j in range(together):
                    total = total + mix(
                        dest * chunk_groups + i * together + j, first_tile, count
                    )
                acc[:, lanes] += total
                return c

            lax.fori_loop(0, chunk_groups // together, some, 0)

            @pl.when(k != 0)
            def _():
                data_copy(dest, me, half).start()

            @pl.when(k == 0)
            def _():
                own_copy(half).start()

            return carry

        lax.fori_loop(0, n, one, 0)

    together = min(8, chunk // GROUP)
    stage(0, 1, tiles - 1, together)

    @pl.when(me > 0)
    def _():
        product_copy().wait_recv()

    stage(1, 0, 1, together)

    sq_all[mz] = jnp.sum(acc[...], axis=0, keepdims=True)

    def sq_copy(dest, source):
        return pltpu.make_async_remote_copy(
            src_ref=sq_all.at[mz],
            dst_ref=sq_all.at[source],
            send_sem=sq_send.at[dest],
            recv_sem=sq_recv.at[source],
            device_id={"ch": dest},
        )

    for k in range(1, nz):
        sq_copy(lax.rem(mz + k, nz), mz).start()
    for k in range(1, nz):
        sq_copy(mz, lax.rem(mz + k, nz)).wait_recv()
    total = sq_all[0]
    for z in range(1, nz):
        total = total + sq_all[z]
    sc_all[me] = lax.rsqrt(total / D + NORM_EPS)

    def sc_copy(dest, source):
        return pltpu.make_async_remote_copy(
            src_ref=sc_all.at[me],
            dst_ref=sc_all.at[source],
            send_sem=sc_send.at[dest],
            recv_sem=sc_recv.at[source],
            device_id={"ctx": dest},
        )

    for k in range(1, n):
        sc_copy(lax.rem(me + k, n), me).start()
    for k in range(1, n):
        sc_copy(me, lax.rem(me + k, n)).wait_recv()
    scale_ref[...] = sc_all[...]

    def finish(k, carry):
        other = lax.rem(me + k, n)
        for half in (0, 1):
            data_copy(me, other, half).wait_recv()
            data_copy(other, me, half).wait_send()
        sc_copy(other, me).wait_send()
        return carry

    lax.fori_loop(1, n, finish, 0)
    own_copy(0).wait()
    own_copy(1).wait()
    for k in range(1, nz):
        sq_copy(lax.rem(mz + k, nz), mz).wait_send()

    @pl.when(me < n - 1)
    def _():
        raw_copy().wait_send()
        product_copy().wait_send()


def local(
    n, nz, gate_input, key_input, value_input, short_filter, mr_filter, mr_skip, norm_gain, doc_lengths
):
    channels, rows_here = gate_input.shape
    chunk = channels // n
    groups = channels // GROUP
    tiles = rows_here // LANES
    ext = pltpu.VMEM((channels, rows_here + LANES), BF16)
    anywhere = pl.BlockSpec(memory_space=pl.ANY)
    vmem = pl.BlockSpec(memory_space=pltpu.VMEM)
    dma = pltpu.SemaphoreType.DMA
    received, scales = pl.pallas_call(
        functools.partial(kernel, n, nz),
        out_shape=(
            jax.ShapeDtypeStruct((chunk, n * rows_here), BF16),
            jax.ShapeDtypeStruct((n, 1, rows_here), F32),
        ),
        in_specs=[
            anywhere,
            anywhere,
            anywhere,
            anywhere,
            anywhere,
            anywhere,
            pl.BlockSpec(memory_space=pltpu.SMEM),
        ],
        out_specs=(anywhere, vmem),
        scratch_shapes=[
            ext,
            ext,
            ext,
            ext,
            pltpu.VMEM((groups, LANES, LANES), BF16),
            pltpu.VMEM((channels, LANES), F32),
            pltpu.VMEM((tiles, 2 * LANES, LANES), BF16),
            pltpu.VMEM((8, rows_here), F32),
            pltpu.VMEM((channels, rows_here), BF16),
            pltpu.VMEM((16, channels), BF16),
            pltpu.VMEM((16, channels), BF16),
            pltpu.VMEM((8, rows_here), F32),
            pltpu.VMEM((nz, 1, rows_here), F32),
            pltpu.VMEM((n, 1, rows_here), F32),
            pltpu.VMEM((3, SHORT, channels), F32),
            pltpu.VMEM((groups, MR), F32),
            pltpu.VMEM((1, channels), F32),
            dma((3,)),
            dma((channels // BLOCK, 3)),
            dma((2,)),
            dma((2,)),
            dma((n, 2)),
            dma((n, 2)),
            dma((nz,)),
            dma((nz,)),
            dma((n,)),
            dma((n,)),
        ],
        compiler_params=pltpu.CompilerParams(
            collective_id=0, has_side_effects=True, vmem_limit_bytes=60 * 1024 * 1024
        ),
        cost_estimate=pl.CostEstimate(
            flops=channels * rows_here * 600, bytes_accessed=channels * rows_here * 8, transcendentals=0
        ),
    )(
        gate_input,
        key_input,
        value_input,
        short_filter,
        mr_filter,
        mr_skip.reshape(1, channels),
        doc_lengths,
    )
    gain_here = lax.dynamic_slice_in_dim(norm_gain, lax.axis_index("ctx") * chunk, chunk)
    row_scale = scales.reshape(1, n * rows_here)
    return (received.astype(F32) * row_scale * gain_here[:, None]).astype(BF16)


def solution(mesh):
    n, nz = mesh.shape["ctx"], mesh.shape["ch"]
    in_specs = (
        P("ch", "ctx"),
        P("ch", "ctx"),
        P("ch", "ctx"),
        P(None, None, "ch"),
        P("ch", None),
        P("ch"),
        P("ch"),
        P(),
    )
    out_specs = P(("ch", "ctx"), None)
    return jax.shard_map(
        functools.partial(local, n, nz), mesh=mesh, in_specs=in_specs, out_specs=out_specs, check_vma=False
    )
```

```python
import functools

import jax
import jax.numpy as jnp
from jax import lax
from jax.experimental import pallas as pl
from jax.experimental.pallas import tpu as pltpu
from jax.sharding import PartitionSpec as P

D = 8192
GROUP = 16
SHORT = 3
MR = 128
NORM_EPS = 1e-06

LANES = 128
F32 = jnp.float32
BF16 = jnp.bfloat16


def short_conv(ext_ref, coef_ref, rows, first_tile, tiles, which, m1, m2):
    width = (tiles + 1) * LANES
    x = ext_ref[rows, first_tile * LANES : first_tile * LANES + width].astype(F32)
    x1 = pltpu.roll(x, 1, 1)[:, LANES:]
    x2 = pltpu.roll(x, 2, 1)[:, LANES:]
    base = which * SHORT
    c0 = coef_ref[rows, base : base + 1]
    c1 = coef_ref[rows, base + 1 : base + 2]
    c2 = coef_ref[rows, base + 2 : base + 3]
    return c0 * x[:, LANES:] + c1 * (x1 * m1) + c2 * (x2 * m2)


def kernel(
    n,
    nz,
    gate_hbm,
    key_hbm,
    value_hbm,
    sf_hbm,
    mr_hbm,
    skip_hbm,
    gain_hbm,
    docs_ref,
    recv_ref,
    scale_ref,
    g_ext,
    k_ext,
    v_ext,
    p_ext,
    circ,
    coef,
    masks,
    lagmask,
    sendbuf,
    raw_send,
    raw_recv,
    acc,
    sq_all,
    sc_all,
    sf_ref,
    mr_ref,
    skip_ref,
    gain_ref,
    small_sem,
    load_sem,
    halo_send,
    halo_recv,
    data_send,
    data_recv,
    sq_send,
    sq_recv,
    sc_send,
    sc_recv,
):
    me = lax.axis_index("ctx")
    mz = lax.axis_index("ch")
    channels, rows_here = gate_hbm.shape
    chunk = channels // n
    groups = channels // GROUP
    tiles = rows_here // LANES
    chunk_groups = chunk // GROUP
    barrier = pltpu.get_barrier_semaphore()

    def offset(step):
        odd = (step + n // 2 + 1) // n
        return ((2 * (step + 1) + 3 * odd) % n) * (1 - (step + 1) // n)

    def load(b, which):
        source = (gate_hbm, key_hbm, value_hbm)[which]
        target = (g_ext, k_ext, v_ext)[which]
        span = pl.ds(pl.multiple_of(b * chunk, chunk), chunk)
        return pltpu.make_async_copy(
            source.at[span, :],
            target.at[span, LANES : LANES + rows_here],
            load_sem.at[b, which],
        )

    small = [
        pltpu.make_async_copy(source, target, small_sem.at[i])
        for i, (source, target) in enumerate(
            ((sf_hbm, sf_ref), (skip_hbm, skip_ref), (gain_hbm, gain_ref), (mr_hbm, mr_ref))
        )
    ]
    for copy in small:
        copy.start()
    for step in range(n):
        dest = lax.rem(me + offset(step), n)
        for which in (1, 2, 0):
            load(dest, which).start()
    for k in range(1, n):
        pl.semaphore_signal(barrier, inc=1, device_id={"ctx": lax.rem(me + k, n)})
    for k in range(1, nz):
        pl.semaphore_signal(barrier, inc=1, device_id={"ch": lax.rem(mz + k, nz)})

    positions = me * rows_here + lax.broadcasted_iota(jnp.int32, (1, rows_here), 1)
    starts = jnp.zeros((1, rows_here), jnp.int32)
    first = jnp.int32(0)
    for d in range(docs_ref.shape[0]):
        starts = jnp.where(positions >= first, first, starts)
        first = first + docs_ref[d]
    for lag in (1, 2):
        lagmask[lag : lag + 1, :] = jnp.where(positions - lag >= starts, 1.0, 0.0).astype(F32)
    s_index = lax.broadcasted_iota(jnp.int32, (LANES, LANES), 0)
    t_index = lax.broadcasted_iota(jnp.int32, (LANES, LANES), 1)
    for tile in range(tiles):
        start_row = starts[:, tile * LANES : (tile + 1) * LANES]
        here = me * rows_here + tile * LANES + s_index
        before = (t_index < s_index) & (here - LANES >= start_row)
        within = (t_index >= s_index) & (here >= start_row)
        masks[tile, 0:LANES, :] = jnp.where(before, 1.0, 0.0).astype(BF16)
        masks[tile, LANES : 2 * LANES, :] = jnp.where(within, 1.0, 0.0).astype(BF16)

    for copy in small:
        copy.wait()

    for b in range(channels // LANES):
        span = slice(b * LANES, (b + 1) * LANES)
        parts = [sf_ref[a, :, span] for a in range(3)] + [skip_ref[:, span], gain_ref[:, span]]
        parts.append(jnp.zeros((5, LANES), F32))
        coef[span, 0:16] = jnp.concatenate(parts, axis=0).T

    row16 = lax.broadcasted_iota(jnp.int32, (16, LANES), 0)
    lane16 = lax.broadcasted_iota(jnp.int32, (16, LANES), 1)

    def pick(which):
        hit = (lane16 - (LANES - 2) == row16 - 2 * which) & (lane16 >= LANES - 2)
        return jnp.where(hit, 1.0, 0.0).astype(BF16)

    last = tiles * LANES

    right = lax.rem(me + 1, n)

    def chunk_rows(c):
        return pl.ds(pl.multiple_of(c * chunk, chunk), chunk)

    def raw_copy(c):
        return pltpu.make_async_remote_copy(
            src_ref=raw_send.at[c],
            dst_ref=raw_recv.at[c],
            send_sem=halo_send.at[c, 0],
            recv_sem=halo_recv.at[c, 0],
            device_id={"ctx": right},
        )

    def product_copy(c):
        return pltpu.make_async_remote_copy(
            src_ref=p_ext.at[chunk_rows(c), last : last + LANES],
            dst_ref=p_ext.at[chunk_rows(c), 0:LANES],
            send_sem=halo_send.at[c, 1],
            recv_sem=halo_recv.at[c, 1],
            device_id={"ctx": right},
        )

    @pl.when(me == 0)
    def _():
        raw_recv[...] = jnp.zeros(raw_recv.shape, BF16)
        p_ext[:, 0:LANES] = jnp.zeros((channels, LANES), BF16)

    def take_raw(c):
        columns = jnp.zeros((16, chunk), F32)
        for which, ref in enumerate((g_ext, k_ext, v_ext)):
            columns = columns + lax.dot_general(
                pick(which),
                ref[chunk_rows(c), last : last + LANES],
                (((1,), (1,)), ((), ())),
                preferred_element_type=F32,
            )
        raw_send[c] = columns.astype(BF16)

    def spread_raw(c):
        for which, ref in enumerate((g_ext, k_ext, v_ext)):
            ref[chunk_rows(c), 0:LANES] = lax.dot_general(
                raw_recv[c],
                pick(which),
                (((0,), (0,)), ((), ())),
                preferred_element_type=F32,
            ).astype(BF16)

    def build(g):
        taps = jnp.broadcast_to(mr_ref[pl.ds(g, 1), :], (LANES, LANES))
        circ[g] = pltpu.roll(taps, 0, 1, stride=1, stride_axis=0).astype(BF16)

    def products(g, first_tile, count):
        rows = pl.ds(pl.multiple_of(g * GROUP, GROUP), GROUP)
        lanes = slice(first_tile * LANES, (first_tile + count) * LANES)
        m1, m2 = lagmask[1:2, lanes], lagmask[2:3, lanes]
        kc = short_conv(k_ext, coef, rows, first_tile, count, 1, m1, m2)
        vc = short_conv(v_ext, coef, rows, first_tile, count, 2, m1, m2)
        p_ext[rows, (first_tile + 1) * LANES : (first_tile + 1 + count) * LANES] = (kc * vc).astype(BF16)

    acc[...] = jnp.zeros(acc.shape, F32)

    def mix(g, first_tile, count):
        rows = pl.ds(pl.multiple_of(g * GROUP, GROUP), GROUP)
        lanes = slice(first_tile * LANES, (first_tile + count) * LANES)
        c = circ[g]
        pair = jnp.concatenate([c, c], axis=0)
        parts = []
        for tile in range(first_tile, first_tile + count):
            parts.append(
                jnp.dot(
                    p_ext[rows, tile * LANES : (tile + 2) * LANES],
                    pair * masks[tile],
                    preferred_element_type=F32,
                )
            )
        mixed = parts[0] if count == 1 else jnp.concatenate(parts, axis=1)
        direct = p_ext[rows, (first_tile + 1) * LANES : (first_tile + 1 + count) * LANES]
        mixed = mixed + coef[rows, 9:10] * direct.astype(F32)
        gate = short_conv(
            g_ext, coef, rows, first_tile, count, 0, lagmask[1:2, lanes], lagmask[2:3, lanes]
        )
        gated = gate * mixed
        sendbuf[rows, lanes] = (gated * coef[rows, 10:11]).astype(BF16)
        squares = gated * gated
        return squares[0:8] + squares[8:16]

    late = (tiles // 2) * LANES

    def data_copy(dest, source, half):
        lanes = (late, last - late) if half == 0 else (0, late)
        return pltpu.make_async_remote_copy(
            src_ref=sendbuf.at[
                pl.ds(pl.multiple_of(dest * chunk, chunk), chunk), lanes[0] : lanes[0] + lanes[1]
            ],
            dst_ref=recv_ref.at[
                :, pl.ds(pl.multiple_of(source * rows_here + lanes[0], LANES), lanes[1])
            ],
            send_sem=data_send.at[dest, half],
            recv_sem=data_recv.at[source, half],
            device_id={"ctx": dest},
        )

    def own_copy(half):
        lanes = (late, last - late) if half == 0 else (0, late)
        return pltpu.make_async_copy(
            sendbuf.at[
                pl.ds(pl.multiple_of(me * chunk, chunk), chunk), lanes[0] : lanes[0] + lanes[1]
            ],
            recv_ref.at[:, pl.ds(pl.multiple_of(me * rows_here + lanes[0], LANES), lanes[1])],
            data_send.at[me, half],
        )

    def stage(half, first_tile, count):
        lanes = slice(first_tile * LANES, (first_tile + count) * LANES)
        together = min(16, chunk_groups)
        unroll = min(8, chunk_groups)

        def one(step, carry):
            k = offset(step)
            dest = lax.rem(me + k, n)
            first_group = dest * chunk_groups
            if half == 0:
                for which in (1, 2, 0):
                    load(dest, which).wait()

                def early(i, c):
                    build(first_group + i)
                    products(first_group + i, 1, tiles - 1)
                    return c

                lax.fori_loop(0, chunk_groups, early, 0, unroll=unroll)
                take_raw(dest)

                @pl.when(step == 0)
                def _():
                    pl.semaphore_wait(barrier, n - 1 + nz - 1)

                @pl.when(me < n - 1)
                def _():
                    raw_copy(dest).start()
                    product_copy(dest).start()

            else:

                @pl.when(me > 0)
                def _():
                    raw_copy(dest).wait_recv()
                    product_copy(dest).wait_recv()

                spread_raw(dest)

                def rest(i, c):
                    products(first_group + i, 0, 1)
                    return c

                lax.fori_loop(0, chunk_groups, rest, 0, unroll=unroll)

            def some(i, c):
                total = jnp.zeros((8, count * LANES), F32)
                for j in range(together):
                    total = total + mix(first_group + i * together + j, first_tile, count)
                acc[:, lanes] += total
                return c

            lax.fori_loop(0, chunk_groups // together, some, 0)

            @pl.when(k != 0)
            def _():
                data_copy(dest, me, half).start()

            @pl.when(k == 0)
            def _():
                own_copy(half).start()

            return carry

        lax.fori_loop(0, n, one, 0)

    stage(0, tiles // 2, tiles - tiles // 2)
    stage(1, 0, tiles // 2)

    sq_all[mz] = jnp.sum(acc[...], axis=0, keepdims=True)

    def sq_copy(dest, source):
        return pltpu.make_async_remote_copy(
            src_ref=sq_all.at[mz],
            dst_ref=sq_all.at[source],
            send_sem=sq_send.at[dest],
            recv_sem=sq_recv.at[source],
            device_id={"ch": dest},
        )

    for k in range(1, nz):
        sq_copy(lax.rem(mz + k, nz), mz).start()
    for k in range(1, nz):
        sq_copy(mz, lax.rem(mz + k, nz)).wait_recv()
    total = sq_all[0]
    for z in range(1, nz):
        total = total + sq_all[z]
    sc_all[me] = lax.rsqrt(total / D + NORM_EPS)

    def sc_copy(dest, source):
        return pltpu.make_async_remote_copy(
            src_ref=sc_all.at[me],
            dst_ref=sc_all.at[source],
            send_sem=sc_send.at[dest],
            recv_sem=sc_recv.at[source],
            device_id={"ctx": dest},
        )

    for k in range(1, n):
        sc_copy(lax.rem(me + k, n), me).start()
    for k in range(1, n):
        sc_copy(me, lax.rem(me + k, n)).wait_recv()
    scale_ref[...] = sc_all[...]

    def finish(k, carry):
        other = lax.rem(me + k, n)
        for half in (0, 1):
            data_copy(me, other, half).wait_recv()
            data_copy(other, me, half).wait_send()
        sc_copy(other, me).wait_send()
        return carry

    lax.fori_loop(1, n, finish, 0)
    own_copy(0).wait()
    own_copy(1).wait()
    for k in range(1, nz):
        sq_copy(lax.rem(mz + k, nz), mz).wait_send()

    @pl.when(me < n - 1)
    def _():
        def sent(c, carry):
            raw_copy(c).wait_send()
            product_copy(c).wait_send()
            return carry

        lax.fori_loop(0, n, sent, 0)


def local(
    n, nz, gate_input, key_input, value_input, short_filter, mr_filter, mr_skip, norm_gain, doc_lengths
):
    channels, rows_here = gate_input.shape
    chunk = channels // n
    groups = channels // GROUP
    tiles = rows_here // LANES
    ext = pltpu.VMEM((channels, rows_here + LANES), BF16)
    anywhere = pl.BlockSpec(memory_space=pl.ANY)
    hbm = pl.BlockSpec(memory_space=pltpu.HBM)
    vmem = pl.BlockSpec(memory_space=pltpu.VMEM)
    dma = pltpu.SemaphoreType.DMA
    received, scales = pl.pallas_call(
        functools.partial(kernel, n, nz),
        out_shape=(
            jax.ShapeDtypeStruct((chunk, n * rows_here), BF16),
            jax.ShapeDtypeStruct((n, 1, rows_here), F32),
        ),
        in_specs=[hbm] * 7 + [pl.BlockSpec(memory_space=pltpu.SMEM)],
        out_specs=(anywhere, vmem),
        scratch_shapes=[
            ext,
            ext,
            ext,
            ext,
            pltpu.VMEM((groups, LANES, LANES), BF16),
            pltpu.VMEM((channels, LANES), F32),
            pltpu.VMEM((tiles, 2 * LANES, LANES), BF16),
            pltpu.VMEM((8, rows_here), F32),
            pltpu.VMEM((channels, rows_here), BF16),
            pltpu.VMEM((n, 16, chunk), BF16),
            pltpu.VMEM((n, 16, chunk), BF16),
            pltpu.VMEM((8, rows_here), F32),
            pltpu.VMEM((nz, 1, rows_here), F32),
            pltpu.VMEM((n, 1, rows_here), F32),
            pltpu.VMEM((3, SHORT, channels), F32),
            pltpu.VMEM((groups, MR), F32),
            pltpu.VMEM((1, channels), F32),
            pltpu.VMEM((1, channels), F32),
            dma((4,)),
            dma((n, 3)),
            dma((n, 2)),
            dma((n, 2)),
            dma((n, 2)),
            dma((n, 2)),
            dma((nz,)),
            dma((nz,)),
            dma((n,)),
            dma((n,)),
        ],
        compiler_params=pltpu.CompilerParams(
            collective_id=0, has_side_effects=True, vmem_limit_bytes=56 * 1024 * 1024
        ),
        cost_estimate=pl.CostEstimate(
            flops=channels * rows_here * 600, bytes_accessed=channels * rows_here * 8, transcendentals=0
        ),
    )(
        gate_input,
        key_input,
        value_input,
        short_filter,
        mr_filter,
        mr_skip.reshape(1, channels),
        norm_gain.reshape(1, channels),
        doc_lengths,
    )
    row_scale = scales.reshape(1, n * rows_here)
    return (received.astype(F32) * row_scale).astype(BF16)


def solution(mesh):
    n, nz = mesh.shape["ctx"], mesh.shape["ch"]
    in_specs = (
        P("ch", "ctx"),
        P("ch", "ctx"),
        P("ch", "ctx"),
        P(None, None, "ch"),
        P("ch", None),
        P("ch"),
        P("ch"),
        P(),
    )
    out_specs = P(("ch", "ctx"), None)
    return jax.shard_map(
        functools.partial(local, n, nz), mesh=mesh, in_specs=in_specs, out_specs=out_specs, check_vma=False
    )
```

```python
import functools

import jax
import jax.numpy as jnp
from jax import lax
from jax.experimental import pallas as pl
from jax.experimental.pallas import tpu as pltpu
from jax.sharding import PartitionSpec as P

D = 8192
GROUP = 16
SHORT = 3
MR = 128
NORM_EPS = 1e-06

LANES = 128
F32 = jnp.float32
BF16 = jnp.bfloat16


def short_conv(ext_ref, coef_ref, rows, first_tile, tiles, which, m1, m2):
    width = (tiles + 1) * LANES
    x = ext_ref[rows, first_tile * LANES : first_tile * LANES + width].astype(F32)
    x1 = pltpu.roll(x, 1, 1)[:, LANES:]
    x2 = pltpu.roll(x, 2, 1)[:, LANES:]
    base = which * SHORT
    c0 = coef_ref[rows, base : base + 1]
    c1 = coef_ref[rows, base + 1 : base + 2]
    c2 = coef_ref[rows, base + 2 : base + 3]
    return c0 * x[:, LANES:] + c1 * (x1 * m1) + c2 * (x2 * m2)


def kernel(
    n,
    nz,
    gate_hbm,
    key_hbm,
    value_hbm,
    sf_hbm,
    mr_hbm,
    skip_hbm,
    gain_hbm,
    docs_ref,
    recv_ref,
    scale_ref,
    g_ext,
    k_ext,
    v_ext,
    p_ext,
    circ,
    coef,
    masks,
    lagmask,
    sendbuf,
    raw_send,
    raw_recv,
    acc,
    sq_all,
    sc_all,
    sf_ref,
    mr_ref,
    skip_ref,
    gain_ref,
    small_sem,
    load_sem,
    halo_send,
    halo_recv,
    data_send,
    data_recv,
    sq_send,
    sq_recv,
    sc_send,
    sc_recv,
):
    me = lax.axis_index("ctx")
    mz = lax.axis_index("ch")
    channels, rows_here = gate_hbm.shape
    chunk = channels // n
    groups = channels // GROUP
    tiles = rows_here // LANES
    chunk_groups = chunk // GROUP
    barrier = pltpu.get_barrier_semaphore()

    def offset(step):
        odd = (step + n // 2 + 1) // n
        return ((2 * (step + 1) + 3 * odd) % n) * (1 - (step + 1) // n)

    def load(b, which):
        source = (gate_hbm, key_hbm, value_hbm)[which]
        target = (g_ext, k_ext, v_ext)[which]
        span = pl.ds(pl.multiple_of(b * chunk, chunk), chunk)
        return pltpu.make_async_copy(
            source.at[span, :],
            target.at[span, LANES : LANES + rows_here],
            load_sem.at[b, which],
        )

    small = [
        pltpu.make_async_copy(source, target, small_sem.at[i])
        for i, (source, target) in enumerate(
            ((sf_hbm, sf_ref), (skip_hbm, skip_ref), (gain_hbm, gain_ref), (mr_hbm, mr_ref))
        )
    ]
    for copy in small:
        copy.start()
    for step in range(n):
        dest = lax.rem(me + offset(step), n)
        for which in (1, 2, 0):
            load(dest, which).start()
    for k in range(1, n):
        pl.semaphore_signal(barrier, inc=1, device_id={"ctx": lax.rem(me + k, n)})
    for k in range(1, nz):
        pl.semaphore_signal(barrier, inc=1, device_id={"ch": lax.rem(mz + k, nz)})

    positions = me * rows_here + lax.broadcasted_iota(jnp.int32, (1, rows_here), 1)
    starts = jnp.zeros((1, rows_here), jnp.int32)
    first = jnp.int32(0)
    for d in range(docs_ref.shape[0]):
        starts = jnp.where(positions >= first, first, starts)
        first = first + docs_ref[d]
    for lag in (1, 2):
        lagmask[lag : lag + 1, :] = jnp.where(positions - lag >= starts, 1.0, 0.0).astype(F32)
    s_index = lax.broadcasted_iota(jnp.int32, (LANES, LANES), 0)
    t_index = lax.broadcasted_iota(jnp.int32, (LANES, LANES), 1)
    for tile in range(tiles):
        start_row = starts[:, tile * LANES : (tile + 1) * LANES]
        here = me * rows_here + tile * LANES + s_index
        before = (t_index < s_index) & (here - LANES >= start_row)
        within = (t_index >= s_index) & (here >= start_row)
        masks[tile, 0:LANES, :] = jnp.where(before, 1.0, 0.0).astype(BF16)
        masks[tile, LANES : 2 * LANES, :] = jnp.where(within, 1.0, 0.0).astype(BF16)

    for copy in small:
        copy.wait()

    for b in range(channels // LANES):
        span = slice(b * LANES, (b + 1) * LANES)
        parts = [sf_ref[a, :, span] for a in range(3)] + [skip_ref[:, span], gain_ref[:, span]]
        parts.append(jnp.zeros((5, LANES), F32))
        coef[span, 0:16] = jnp.concatenate(parts, axis=0).T

    row16 = lax.broadcasted_iota(jnp.int32, (16, LANES), 0)
    lane16 = lax.broadcasted_iota(jnp.int32, (16, LANES), 1)

    def pick(which):
        hit = (lane16 - (LANES - 2) == row16 - 2 * which) & (lane16 >= LANES - 2)
        return jnp.where(hit, 1.0, 0.0).astype(BF16)

    last = tiles * LANES

    right = lax.rem(me + 1, n)

    def chunk_rows(c):
        return pl.ds(pl.multiple_of(c * chunk, chunk), chunk)

    def raw_copy(c):
        return pltpu.make_async_remote_copy(
            src_ref=raw_send.at[c],
            dst_ref=raw_recv.at[c],
            send_sem=halo_send.at[c, 0],
            recv_sem=halo_recv.at[c, 0],
            device_id={"ctx": right},
        )

    def product_copy(c):
        return pltpu.make_async_remote_copy(
            src_ref=p_ext.at[chunk_rows(c), last : last + LANES],
            dst_ref=p_ext.at[chunk_rows(c), 0:LANES],
            send_sem=halo_send.at[c, 1],
            recv_sem=halo_recv.at[c, 1],
            device_id={"ctx": right},
        )

    @pl.when(me == 0)
    def _():
        raw_recv[...] = jnp.zeros(raw_recv.shape, BF16)
        p_ext[:, 0:LANES] = jnp.zeros((channels, LANES), BF16)

    def take_raw(c):
        columns = jnp.zeros((16, chunk), F32)
        for which, ref in enumerate((g_ext, k_ext, v_ext)):
            columns = columns + lax.dot_general(
                pick(which),
                ref[chunk_rows(c), last : last + LANES],
                (((1,), (1,)), ((), ())),
                preferred_element_type=F32,
            )
        raw_send[c] = columns.astype(BF16)

    def spread_raw(c):
        for which, ref in enumerate((g_ext, k_ext, v_ext)):
            ref[chunk_rows(c), 0:LANES] = lax.dot_general(
                raw_recv[c],
                pick(which),
                (((0,), (0,)), ((), ())),
                preferred_element_type=F32,
            ).astype(BF16)

    def build(g):
        taps = jnp.broadcast_to(mr_ref[pl.ds(g, 1), :], (LANES, LANES))
        circ[g] = pltpu.roll(taps, 0, 1, stride=1, stride_axis=0).astype(BF16)

    def products(g, first_tile, count):
        rows = pl.ds(pl.multiple_of(g * GROUP, GROUP), GROUP)
        lanes = slice(first_tile * LANES, (first_tile + count) * LANES)
        m1, m2 = lagmask[1:2, lanes], lagmask[2:3, lanes]
        kc = short_conv(k_ext, coef, rows, first_tile, count, 1, m1, m2)
        vc = short_conv(v_ext, coef, rows, first_tile, count, 2, m1, m2)
        p_ext[rows, (first_tile + 1) * LANES : (first_tile + 1 + count) * LANES] = (kc * vc).astype(BF16)

    acc[...] = jnp.zeros(acc.shape, F32)

    def mix(g, first_tile, count):
        rows = pl.ds(pl.multiple_of(g * GROUP, 2 * GROUP), 2 * GROUP)
        lanes = slice(first_tile * LANES, (first_tile + count) * LANES)
        both = jnp.concatenate([circ[g], circ[g + 1]], axis=1)
        pair = jnp.concatenate([both, both], axis=0)
        parts = []
        for tile in range(first_tile, first_tile + count):
            mask = masks[tile]
            result = jnp.dot(
                p_ext[rows, tile * LANES : (tile + 2) * LANES],
                pair * jnp.concatenate([mask, mask], axis=1),
                preferred_element_type=F32,
            )
            parts.append(
                jnp.concatenate([result[:GROUP, :LANES], result[GROUP:, LANES:]], axis=0)
            )
        mixed = parts[0] if count == 1 else jnp.concatenate(parts, axis=1)
        direct = p_ext[rows, (first_tile + 1) * LANES : (first_tile + 1 + count) * LANES]
        mixed = mixed + coef[rows, 9:10] * direct.astype(F32)
        gate = short_conv(
            g_ext, coef, rows, first_tile, count, 0, lagmask[1:2, lanes], lagmask[2:3, lanes]
        )
        gated = gate * mixed
        sendbuf[rows, lanes] = (gated * coef[rows, 10:11]).astype(BF16)
        squares = gated * gated
        return squares[0:8] + squares[8:16] + squares[16:24] + squares[24:32]

    late = (tiles // 2) * LANES

    def data_copy(dest, source, half):
        lanes = (late, last - late) if half == 0 else (0, late)
        return pltpu.make_async_remote_copy(
            src_ref=sendbuf.at[
                pl.ds(pl.multiple_of(dest * chunk, chunk), chunk), lanes[0] : lanes[0] + lanes[1]
            ],
            dst_ref=recv_ref.at[
                :, pl.ds(pl.multiple_of(source * rows_here + lanes[0], LANES), lanes[1])
            ],
            send_sem=data_send.at[dest, half],
            recv_sem=data_recv.at[source, half],
            device_id={"ctx": dest},
        )

    def own_copy(half):
        lanes = (late, last - late) if half == 0 else (0, late)
        return pltpu.make_async_copy(
            sendbuf.at[
                pl.ds(pl.multiple_of(me * chunk, chunk), chunk), lanes[0] : lanes[0] + lanes[1]
            ],
            recv_ref.at[:, pl.ds(pl.multiple_of(me * rows_here + lanes[0], LANES), lanes[1])],
            data_send.at[me, half],
        )

    def stage(half, first_tile, count):
        lanes = slice(first_tile * LANES, (first_tile + count) * LANES)
        together = min(16, chunk_groups)
        unroll = min(8, chunk_groups)

        def one(step, carry):
            k = offset(step)
            dest = lax.rem(me + k, n)
            first_group = dest * chunk_groups
            if half == 0:
                for which in (1, 2, 0):
                    load(dest, which).wait()

                def early(i, c):
                    build(first_group + i)
                    products(first_group + i, 1, tiles - 1)
                    return c

                lax.fori_loop(0, chunk_groups, early, 0, unroll=unroll)
                take_raw(dest)

                @pl.when(step == 0)
                def _():
                    pl.semaphore_wait(barrier, n - 1 + nz - 1)

                @pl.when(me < n - 1)
                def _():
                    raw_copy(dest).start()
                    product_copy(dest).start()

            else:

                @pl.when(me > 0)
                def _():
                    raw_copy(dest).wait_recv()
                    product_copy(dest).wait_recv()

                spread_raw(dest)

                def rest(i, c):
                    products(first_group + i, 0, 1)
                    return c

                lax.fori_loop(0, chunk_groups, rest, 0, unroll=unroll)

            def some(i, c):
                total = jnp.zeros((8, count * LANES), F32)
                for j in range(0, together, 2):
                    total = total + mix(first_group + i * together + j, first_tile, count)
                acc[:, lanes] += total
                return c

            lax.fori_loop(0, chunk_groups // together, some, 0)

            @pl.when(k != 0)
            def _():
                data_copy(dest, me, half).start()

            @pl.when(k == 0)
            def _():
                own_copy(half).start()

            return carry

        lax.fori_loop(0, n, one, 0)

    stage(0, tiles // 2, tiles - tiles // 2)
    stage(1, 0, tiles // 2)

    sq_all[mz] = jnp.sum(acc[...], axis=0, keepdims=True)

    def sq_copy(dest, source):
        return pltpu.make_async_remote_copy(
            src_ref=sq_all.at[mz],
            dst_ref=sq_all.at[source],
            send_sem=sq_send.at[dest],
            recv_sem=sq_recv.at[source],
            device_id={"ch": dest},
        )

    for k in range(1, nz):
        sq_copy(lax.rem(mz + k, nz), mz).start()
    for k in range(1, nz):
        sq_copy(mz, lax.rem(mz + k, nz)).wait_recv()
    total = sq_all[0]
    for z in range(1, nz):
        total = total + sq_all[z]
    sc_all[me] = lax.rsqrt(total / D + NORM_EPS)

    def sc_copy(dest, source):
        return pltpu.make_async_remote_copy(
            src_ref=sc_all.at[me],
            dst_ref=sc_all.at[source],
            send_sem=sc_send.at[dest],
            recv_sem=sc_recv.at[source],
            device_id={"ctx": dest},
        )

    for k in range(1, n):
        sc_copy(lax.rem(me + k, n), me).start()
    for k in range(1, n):
        sc_copy(me, lax.rem(me + k, n)).wait_recv()
    scale_ref[...] = sc_all[...]

    def finish(k, carry):
        other = lax.rem(me + k, n)
        for half in (0, 1):
            data_copy(me, other, half).wait_recv()
            data_copy(other, me, half).wait_send()
        sc_copy(other, me).wait_send()
        return carry

    lax.fori_loop(1, n, finish, 0)
    own_copy(0).wait()
    own_copy(1).wait()
    for k in range(1, nz):
        sq_copy(lax.rem(mz + k, nz), mz).wait_send()

    @pl.when(me < n - 1)
    def _():
        def sent(c, carry):
            raw_copy(c).wait_send()
            product_copy(c).wait_send()
            return carry

        lax.fori_loop(0, n, sent, 0)


def scale_kernel(source, scales, target, held, scaled, load_sem, store_sem):
    n, _, width = scales.shape
    parts = load_sem.shape[0]
    height = source.shape[0] // parts
    spans = [slice(i * height, (i + 1) * height) for i in range(parts)]
    loads = [pltpu.make_async_copy(source.at[r], held.at[r], load_sem.at[i]) for i, r in enumerate(spans)]
    stores = [pltpu.make_async_copy(scaled.at[r], target.at[r], store_sem.at[i]) for i, r in enumerate(spans)]
    for load in loads:
        load.start()
    for load, store, rows in zip(loads, stores, spans):
        load.wait()
        for i in range(n):
            lanes = slice(i * width, (i + 1) * width)
            scaled[rows, lanes] = (held[rows, lanes].astype(F32) * scales[i]).astype(BF16)
        store.start()
    for store in stores:
        store.wait()


def local(
    n, nz, gate_input, key_input, value_input, short_filter, mr_filter, mr_skip, norm_gain, doc_lengths
):
    channels, rows_here = gate_input.shape
    chunk = channels // n
    groups = channels // GROUP
    tiles = rows_here // LANES
    ext = pltpu.VMEM((channels, rows_here + LANES), BF16)
    anywhere = pl.BlockSpec(memory_space=pl.ANY)
    hbm = pl.BlockSpec(memory_space=pltpu.HBM)
    vmem = pl.BlockSpec(memory_space=pltpu.VMEM)
    dma = pltpu.SemaphoreType.DMA
    received, scales = pl.pallas_call(
        functools.partial(kernel, n, nz),
        out_shape=(
            jax.ShapeDtypeStruct((chunk, n * rows_here), BF16),
            jax.ShapeDtypeStruct((n, 1, rows_here), F32),
        ),
        in_specs=[hbm] * 7 + [pl.BlockSpec(memory_space=pltpu.SMEM)],
        out_specs=(anywhere, vmem),
        scratch_shapes=[
            ext,
            ext,
            ext,
            ext,
            pltpu.VMEM((groups, LANES, LANES), BF16),
            pltpu.VMEM((channels, LANES), F32),
            pltpu.VMEM((tiles, 2 * LANES, LANES), BF16),
            pltpu.VMEM((8, rows_here), F32),
            pltpu.VMEM((channels, rows_here), BF16),
            pltpu.VMEM((n, 16, chunk), BF16),
            pltpu.VMEM((n, 16, chunk), BF16),
            pltpu.VMEM((8, rows_here), F32),
            pltpu.VMEM((nz, 1, rows_here), F32),
            pltpu.VMEM((n, 1, rows_here), F32),
            pltpu.VMEM((3, SHORT, channels), F32),
            pltpu.VMEM((groups, MR), F32),
            pltpu.VMEM((1, channels), F32),
            pltpu.VMEM((1, channels), F32),
            dma((4,)),
            dma((n, 3)),
            dma((n, 2)),
            dma((n, 2)),
            dma((n, 2)),
            dma((n, 2)),
            dma((nz,)),
            dma((nz,)),
            dma((n,)),
            dma((n,)),
        ],
        compiler_params=pltpu.CompilerParams(
            collective_id=0, has_side_effects=True, vmem_limit_bytes=56 * 1024 * 1024
        ),
        cost_estimate=pl.CostEstimate(
            flops=channels * rows_here * 600, bytes_accessed=channels * rows_here * 8, transcendentals=0
        ),
    )(
        gate_input,
        key_input,
        value_input,
        short_filter,
        mr_filter,
        mr_skip.reshape(1, channels),
        norm_gain.reshape(1, channels),
        doc_lengths,
    )
    return pl.pallas_call(
        scale_kernel,
        out_shape=jax.ShapeDtypeStruct(received.shape, BF16),
        in_specs=[anywhere, vmem],
        out_specs=anywhere,
        scratch_shapes=[
            pltpu.VMEM(received.shape, BF16),
            pltpu.VMEM(received.shape, BF16),
            dma((chunk // 32,)),
            dma((chunk // 32,)),
        ],
        compiler_params=pltpu.CompilerParams(vmem_limit_bytes=56 * 1024 * 1024),
    )(received, scales)


def solution(mesh):
    n, nz = mesh.shape["ctx"], mesh.shape["ch"]
    in_specs = (
        P("ch", "ctx"),
        P("ch", "ctx"),
        P("ch", "ctx"),
        P(None, None, "ch"),
        P("ch", None),
        P("ch"),
        P("ch"),
        P(),
    )
    out_specs = P(("ch", "ctx"), None)
    return jax.shard_map(
        functools.partial(local, n, nz), mesh=mesh, in_specs=in_specs, out_specs=out_specs, check_vma=False
    )
```

```python
import functools

import jax
import jax.numpy as jnp
from jax import lax
from jax.experimental import pallas as pl
from jax.experimental.pallas import tpu as pltpu
from jax.sharding import PartitionSpec as P

D = 8192
GROUP = 16
SHORT = 3
MR = 128
NORM_EPS = 1e-06

LANES = 128
F32 = jnp.float32
BF16 = jnp.bfloat16


def short_conv(ext_ref, coef_ref, rows, first_tile, tiles, which, m1, m2):
    width = (tiles + 1) * LANES
    x = ext_ref[rows, first_tile * LANES : first_tile * LANES + width].astype(F32)
    x1 = pltpu.roll(x, 1, 1)[:, LANES:]
    x2 = pltpu.roll(x, 2, 1)[:, LANES:]
    base = which * SHORT
    c0 = coef_ref[rows, base : base + 1]
    c1 = coef_ref[rows, base + 1 : base + 2]
    c2 = coef_ref[rows, base + 2 : base + 3]
    return c0 * x[:, LANES:] + c1 * (x1 * m1) + c2 * (x2 * m2)


def kernel(
    n,
    nz,
    gate_hbm,
    key_hbm,
    value_hbm,
    sf_hbm,
    mr_hbm,
    skip_hbm,
    gain_hbm,
    docs_ref,
    recv_ref,
    scale_ref,
    g_ext,
    k_ext,
    v_ext,
    p_ext,
    circ,
    coef,
    masks,
    lagmask,
    sendbuf,
    raw_send,
    raw_recv,
    halo_out,
    halo_in,
    acc,
    sq_all,
    own_scale,
    sf_ref,
    mr_ref,
    skip_ref,
    gain_ref,
    small_sem,
    load_sem,
    halo_send,
    halo_recv,
    data_send,
    data_recv,
    sq_send,
    sq_recv,
    sc_send,
    sc_recv,
):
    me = lax.axis_index("ctx")
    mz = lax.axis_index("ch")
    channels, rows_here = gate_hbm.shape
    chunk = channels // n
    groups = channels // GROUP
    tiles = rows_here // LANES
    chunk_groups = chunk // GROUP
    barrier = pltpu.get_barrier_semaphore()

    def offset(step):
        odd = (step + n // 2 + 1) // n
        return ((2 * (step + 1) + 3 * odd) % n) * (1 - (step + 1) // n)

    def load(b, which):
        source = (gate_hbm, key_hbm, value_hbm)[which]
        target = (g_ext, k_ext, v_ext)[which]
        span = pl.ds(pl.multiple_of(b * chunk, chunk), chunk)
        return pltpu.make_async_copy(
            source.at[span, :],
            target.at[span, LANES : LANES + rows_here],
            load_sem.at[b, which],
        )

    small = [
        pltpu.make_async_copy(source, target, small_sem.at[i])
        for i, (source, target) in enumerate(
            ((sf_hbm, sf_ref), (skip_hbm, skip_ref), (gain_hbm, gain_ref), (mr_hbm, mr_ref))
        )
    ]
    for copy in small:
        copy.start()
    for step in range(n):
        dest = lax.rem(me + offset(step), n)
        for which in (1, 2, 0):
            load(dest, which).start()
    for k in range(1, n):
        pl.semaphore_signal(barrier, inc=1, device_id={"ctx": lax.rem(me + k, n)})
    for k in range(1, nz):
        pl.semaphore_signal(barrier, inc=1, device_id={"ch": lax.rem(mz + k, nz)})

    positions = me * rows_here + lax.broadcasted_iota(jnp.int32, (1, rows_here), 1)
    starts = jnp.zeros((1, rows_here), jnp.int32)
    first = jnp.int32(0)
    for d in range(docs_ref.shape[0]):
        starts = jnp.where(positions >= first, first, starts)
        first = first + docs_ref[d]
    for lag in (1, 2):
        lagmask[lag : lag + 1, :] = jnp.where(positions - lag >= starts, 1.0, 0.0).astype(F32)
    s_index = lax.broadcasted_iota(jnp.int32, (LANES, LANES), 0)
    t_index = lax.broadcasted_iota(jnp.int32, (LANES, LANES), 1)
    for tile in range(tiles):
        start_row = starts[:, tile * LANES : (tile + 1) * LANES]
        here = me * rows_here + tile * LANES + s_index
        before = (t_index < s_index) & (here - LANES >= start_row)
        within = (t_index >= s_index) & (here >= start_row)
        masks[tile, 0:LANES, :] = jnp.where(before, 1.0, 0.0).astype(BF16)
        masks[tile, LANES : 2 * LANES, :] = jnp.where(within, 1.0, 0.0).astype(BF16)

    for copy in small:
        copy.wait()

    for b in range(channels // LANES):
        span = slice(b * LANES, (b + 1) * LANES)
        parts = [sf_ref[a, :, span] for a in range(3)] + [skip_ref[:, span], gain_ref[:, span]]
        parts.append(jnp.zeros((5, LANES), F32))
        coef[span, 0:16] = jnp.concatenate(parts, axis=0).T

    row16 = lax.broadcasted_iota(jnp.int32, (16, LANES), 0)
    lane16 = lax.broadcasted_iota(jnp.int32, (16, LANES), 1)

    def pick(which):
        hit = (lane16 - (LANES - 2) == row16 - 2 * which) & (lane16 >= LANES - 2)
        return jnp.where(hit, 1.0, 0.0).astype(BF16)

    last = tiles * LANES

    right = lax.rem(me + 1, n)

    def chunk_rows(c):
        return pl.ds(pl.multiple_of(c * chunk, chunk), chunk)

    def raw_copy(c):
        return pltpu.make_async_remote_copy(
            src_ref=raw_send.at[c],
            dst_ref=raw_recv.at[c],
            send_sem=halo_send.at[c, 0],
            recv_sem=halo_recv.at[c, 0],
            device_id={"ctx": right},
        )

    def product_copy(c):
        return pltpu.make_async_remote_copy(
            src_ref=halo_out.at[chunk_rows(c)],
            dst_ref=halo_in.at[chunk_rows(c)],
            send_sem=halo_send.at[c, 1],
            recv_sem=halo_recv.at[c, 1],
            device_id={"ctx": right},
        )

    @pl.when(me == 0)
    def _():
        raw_recv[...] = jnp.zeros(raw_recv.shape, BF16)
        halo_in[...] = jnp.zeros(halo_in.shape, BF16)

    def take_raw(c):
        columns = jnp.zeros((16, chunk), F32)
        for which, ref in enumerate((g_ext, k_ext, v_ext)):
            columns = columns + lax.dot_general(
                pick(which),
                ref[chunk_rows(c), last : last + LANES],
                (((1,), (1,)), ((), ())),
                preferred_element_type=F32,
            )
        raw_send[c] = columns.astype(BF16)

    def spread_raw(c):
        for which, ref in enumerate((g_ext, k_ext, v_ext)):
            ref[chunk_rows(c), 0:LANES] = lax.dot_general(
                raw_recv[c],
                pick(which),
                (((0,), (0,)), ((), ())),
                preferred_element_type=F32,
            ).astype(BF16)

    def build(g):
        taps = jnp.broadcast_to(mr_ref[pl.ds(g, 1), :], (LANES, LANES))
        circ[g] = pltpu.roll(taps, 0, 1, stride=1, stride_axis=0).astype(BF16)

    def products(g, first_tile, count):
        rows = pl.ds(pl.multiple_of(g * GROUP, GROUP), GROUP)
        lanes = slice(first_tile * LANES, (first_tile + count) * LANES)
        m1, m2 = lagmask[1:2, lanes], lagmask[2:3, lanes]
        kc = short_conv(k_ext, coef, rows, first_tile, count, 1, m1, m2)
        vc = short_conv(v_ext, coef, rows, first_tile, count, 2, m1, m2)
        result = (kc * vc).astype(BF16)
        p_ext[rows, (first_tile + 1) * LANES : (first_tile + 1 + count) * LANES] = result
        if first_tile + count == tiles:
            halo_out[rows] = result[:, (count - 1) * LANES :]

    acc[...] = jnp.zeros(acc.shape, F32)

    def mix(g, first_tile, count):
        rows = pl.ds(pl.multiple_of(g * GROUP, 2 * GROUP), 2 * GROUP)
        lanes = slice(first_tile * LANES, (first_tile + count) * LANES)
        both = jnp.concatenate([circ[g], circ[g + 1]], axis=1)
        pair = jnp.concatenate([both, both], axis=0)
        parts = []
        for tile in range(first_tile, first_tile + count):
            mask = masks[tile]
            if tile == 0:
                window = jnp.concatenate([halo_in[rows], p_ext[rows, LANES : 2 * LANES]], axis=1)
            else:
                window = p_ext[rows, tile * LANES : (tile + 2) * LANES]
            result = jnp.dot(
                window,
                pair * jnp.concatenate([mask, mask], axis=1),
                preferred_element_type=F32,
            )
            parts.append(
                jnp.concatenate([result[:GROUP, :LANES], result[GROUP:, LANES:]], axis=0)
            )
        mixed = parts[0] if count == 1 else jnp.concatenate(parts, axis=1)
        direct = p_ext[rows, (first_tile + 1) * LANES : (first_tile + 1 + count) * LANES]
        mixed = mixed + coef[rows, 9:10] * direct.astype(F32)
        gate = short_conv(
            g_ext, coef, rows, first_tile, count, 0, lagmask[1:2, lanes], lagmask[2:3, lanes]
        )
        gated = gate * mixed
        sendbuf[0 if first_tile else 1, rows] = (gated * coef[rows, 10:11]).astype(BF16)
        squares = gated * gated
        return squares[0:8] + squares[8:16] + squares[16:24] + squares[24:32]

    def data_copy(dest, source, half):
        return pltpu.make_async_remote_copy(
            src_ref=sendbuf.at[half, chunk_rows(dest)],
            dst_ref=recv_ref.at[source, half],
            send_sem=data_send.at[dest, half],
            recv_sem=data_recv.at[source, half],
            device_id={"ctx": dest},
        )

    def own_copy(half):
        return pltpu.make_async_copy(
            sendbuf.at[half, chunk_rows(me)], recv_ref.at[me, half], data_send.at[me, half]
        )

    def stage(half, first_tile, count):
        lanes = slice(first_tile * LANES, (first_tile + count) * LANES)
        together = min(16, chunk_groups)
        unroll = min(8, chunk_groups)

        def one(step, carry):
            k = offset(step)
            dest = lax.rem(me + k, n)
            first_group = dest * chunk_groups
            if half == 0:
                for which in (1, 2, 0):
                    load(dest, which).wait()

                def early(i, c):
                    build(first_group + i)
                    products(first_group + i, 1, tiles - 1)
                    return c

                lax.fori_loop(0, chunk_groups, early, 0, unroll=unroll)
                take_raw(dest)

                @pl.when(step == 0)
                def _():
                    pl.semaphore_wait(barrier, n - 1 + nz - 1)

                @pl.when(me < n - 1)
                def _():
                    raw_copy(dest).start()
                    product_copy(dest).start()

            else:

                @pl.when(me > 0)
                def _():
                    raw_copy(dest).wait_recv()
                    product_copy(dest).wait_recv()

                spread_raw(dest)

                def rest(i, c):
                    products(first_group + i, 0, 1)
                    return c

                lax.fori_loop(0, chunk_groups, rest, 0, unroll=unroll)

            def some(i, c):
                total = jnp.zeros((8, count * LANES), F32)
                for j in range(0, together, 2):
                    total = total + mix(first_group + i * together + j, first_tile, count)
                acc[:, lanes] += total
                return c

            lax.fori_loop(0, chunk_groups // together, some, 0)

            @pl.when(k != 0)
            def _():
                data_copy(dest, me, half).start()

            @pl.when(k == 0)
            def _():
                own_copy(half).start()

            return carry

        lax.fori_loop(0, n, one, 0)

    stage(0, tiles // 2, tiles - tiles // 2)
    stage(1, 0, tiles // 2)

    sq_all[mz] = jnp.sum(acc[...], axis=0, keepdims=True)

    def sq_copy(dest, source):
        return pltpu.make_async_remote_copy(
            src_ref=sq_all.at[mz],
            dst_ref=sq_all.at[source],
            send_sem=sq_send.at[dest],
            recv_sem=sq_recv.at[source],
            device_id={"ch": dest},
        )

    for k in range(1, nz):
        sq_copy(lax.rem(mz + k, nz), mz).start()
    for k in range(1, nz):
        sq_copy(mz, lax.rem(mz + k, nz)).wait_recv()
    total = sq_all[0]
    for z in range(1, nz):
        total = total + sq_all[z]
    own_scale[0] = lax.rsqrt(total / D + NORM_EPS)
    keep_scale = pltpu.make_async_copy(own_scale.at[0], scale_ref.at[me], sc_send.at[me])
    keep_scale.start()

    def sc_copy(dest, source):
        return pltpu.make_async_remote_copy(
            src_ref=own_scale.at[0],
            dst_ref=scale_ref.at[source],
            send_sem=sc_send.at[dest],
            recv_sem=sc_recv.at[source],
            device_id={"ctx": dest},
        )

    for k in range(1, n):
        sc_copy(lax.rem(me + k, n), me).start()
    for k in range(1, n):
        sc_copy(me, lax.rem(me + k, n)).wait_recv()
    keep_scale.wait()

    def finish(k, carry):
        other = lax.rem(me + k, n)
        for half in (0, 1):
            data_copy(me, other, half).wait_recv()
            data_copy(other, me, half).wait_send()
        sc_copy(other, me).wait_send()
        return carry

    lax.fori_loop(1, n, finish, 0)
    own_copy(0).wait()
    own_copy(1).wait()
    for k in range(1, nz):
        sq_copy(lax.rem(mz + k, nz), mz).wait_send()

    @pl.when(me < n - 1)
    def _():
        def sent(c, carry):
            raw_copy(c).wait_send()
            product_copy(c).wait_send()
            return carry

        lax.fori_loop(0, n, sent, 0)


def scale_kernel(source, scales_hbm, target, held, scaled, scales, scale_sem, load_sem, store_sem):
    n, _, _, width = source.shape
    fetch = pltpu.make_async_copy(scales_hbm, scales, scale_sem)
    fetch.start()
    loads, stores = [], []
    for i in range(n):
        lanes = slice(2 * i * width, 2 * (i + 1) * width)
        loads.append(pltpu.make_async_copy(source.at[i], held.at[i], load_sem.at[i]))
        stores.append(pltpu.make_async_copy(scaled.at[:, lanes], target.at[:, lanes], store_sem.at[i]))
        loads[i].start()
    fetch.wait()
    for i in range(n):
        loads[i].wait()
        for half in range(2):
            first = (2 * i + 1 - half) * width
            scale = scales[i, :, (1 - half) * width : (2 - half) * width]
            scaled[:, first : first + width] = (held[i, half].astype(F32) * scale).astype(BF16)
        stores[i].start()
    for store in stores:
        store.wait()


def local(
    n, nz, gate_input, key_input, value_input, short_filter, mr_filter, mr_skip, norm_gain, doc_lengths
):
    channels, rows_here = gate_input.shape
    chunk = channels // n
    groups = channels // GROUP
    tiles = rows_here // LANES
    ext = pltpu.VMEM((channels, rows_here + LANES), BF16)
    anywhere = pl.BlockSpec(memory_space=pl.ANY)
    hbm = pl.BlockSpec(memory_space=pltpu.HBM)
    dma = pltpu.SemaphoreType.DMA
    received, scales = pl.pallas_call(
        functools.partial(kernel, n, nz),
        out_shape=(
            jax.ShapeDtypeStruct((n, 2, chunk, rows_here // 2), BF16),
            jax.ShapeDtypeStruct((n, 1, rows_here), F32),
        ),
        in_specs=[hbm] * 7 + [pl.BlockSpec(memory_space=pltpu.SMEM)],
        out_specs=(anywhere, anywhere),
        scratch_shapes=[
            ext,
            ext,
            ext,
            ext,
            pltpu.VMEM((groups, LANES, LANES), BF16),
            pltpu.VMEM((channels, LANES), F32),
            pltpu.VMEM((tiles, 2 * LANES, LANES), BF16),
            pltpu.VMEM((8, rows_here), F32),
            pltpu.VMEM((2, channels, rows_here // 2), BF16),
            pltpu.VMEM((n, 16, chunk), BF16),
            pltpu.VMEM((n, 16, chunk), BF16),
            pltpu.VMEM((channels, LANES), BF16),
            pltpu.VMEM((channels, LANES), BF16),
            pltpu.VMEM((8, rows_here), F32),
            pltpu.VMEM((nz, 1, rows_here), F32),
            pltpu.VMEM((1, 1, rows_here), F32),
            pltpu.VMEM((3, SHORT, channels), F32),
            pltpu.VMEM((groups, MR), F32),
            pltpu.VMEM((1, channels), F32),
            pltpu.VMEM((1, channels), F32),
            dma((4,)),
            dma((n, 3)),
            dma((n, 2)),
            dma((n, 2)),
            dma((n, 2)),
            dma((n, 2)),
            dma((nz,)),
            dma((nz,)),
            dma((n,)),
            dma((n,)),
        ],
        compiler_params=pltpu.CompilerParams(
            collective_id=0, has_side_effects=True, vmem_limit_bytes=56 * 1024 * 1024
        ),
        cost_estimate=pl.CostEstimate(
            flops=channels * rows_here * 600, bytes_accessed=channels * rows_here * 8, transcendentals=0
        ),
    )(
        gate_input,
        key_input,
        value_input,
        short_filter,
        mr_filter,
        mr_skip.reshape(1, channels),
        norm_gain.reshape(1, channels),
        doc_lengths,
    )
    return pl.pallas_call(
        scale_kernel,
        out_shape=jax.ShapeDtypeStruct((chunk, n * rows_here), BF16),
        in_specs=[anywhere, anywhere],
        out_specs=anywhere,
        scratch_shapes=[
            pltpu.VMEM(received.shape, BF16),
            pltpu.VMEM((chunk, n * rows_here), BF16),
            pltpu.VMEM(scales.shape, F32),
            dma(()),
            dma((n,)),
            dma((n,)),
        ],
        compiler_params=pltpu.CompilerParams(vmem_limit_bytes=56 * 1024 * 1024),
    )(received, scales)


def solution(mesh):
    n, nz = mesh.shape["ctx"], mesh.shape["ch"]
    in_specs = (
        P("ch", "ctx"),
        P("ch", "ctx"),
        P("ch", "ctx"),
        P(None, None, "ch"),
        P("ch", None),
        P("ch"),
        P("ch"),
        P(),
    )
    out_specs = P(("ch", "ctx"), None)
    return jax.shard_map(
        functools.partial(local, n, nz), mesh=mesh, in_specs=in_specs, out_specs=out_specs, check_vma=False
    )
```

```python
import functools

import jax
import jax.numpy as jnp
from jax import lax
from jax.experimental import pallas as pl
from jax.experimental.pallas import tpu as pltpu
from jax.sharding import PartitionSpec as P

D = 8192
GROUP = 16
SHORT = 3
MR = 128
NORM_EPS = 1e-06

LANES = 128
F32 = jnp.float32
BF16 = jnp.bfloat16


def short_conv(ext_ref, coef_ref, rows, first_tile, tiles, which, m1, m2):
    width = (tiles + 1) * LANES
    x = ext_ref[rows, first_tile * LANES : first_tile * LANES + width].astype(F32)
    x1 = pltpu.roll(x, 1, 1)[:, LANES:]
    x2 = pltpu.roll(x, 2, 1)[:, LANES:]
    base = which * SHORT
    c0 = coef_ref[rows, base : base + 1]
    c1 = coef_ref[rows, base + 1 : base + 2]
    c2 = coef_ref[rows, base + 2 : base + 3]
    return c0 * x[:, LANES:] + c1 * (x1 * m1) + c2 * (x2 * m2)


def kernel(
    n,
    nz,
    gate_hbm,
    key_hbm,
    value_hbm,
    sf_hbm,
    mr_hbm,
    skip_hbm,
    gain_hbm,
    docs_ref,
    recv_ref,
    scale_ref,
    g_ext,
    k_ext,
    v_ext,
    p_ext,
    circ,
    coef,
    masks,
    lagmask,
    sendbuf,
    raw_send,
    raw_recv,
    halo_out,
    halo_in,
    acc,
    sq_all,
    own_scale,
    sf_ref,
    mr_ref,
    skip_ref,
    gain_ref,
    small_sem,
    load_sem,
    halo_send,
    halo_recv,
    data_send,
    data_recv,
    sq_send,
    sq_recv,
    sc_send,
    sc_recv,
):
    me = lax.axis_index("ctx")
    mz = lax.axis_index("ch")
    channels, rows_here = gate_hbm.shape
    chunk = channels // n
    groups = channels // GROUP
    tiles = rows_here // LANES
    chunk_groups = chunk // GROUP
    barrier = pltpu.get_barrier_semaphore()

    def offset(step):
        odd = (step + n // 2 + 1) // n
        return ((2 * (step + 1) + 3 * odd) % n) * (1 - (step + 1) // n)

    def load(b, which):
        source = (gate_hbm, key_hbm, value_hbm)[which]
        target = (g_ext, k_ext, v_ext)[which]
        span = pl.ds(pl.multiple_of(b * chunk, chunk), chunk)
        return pltpu.make_async_copy(
            source.at[span, :],
            target.at[span, LANES : LANES + rows_here],
            load_sem.at[b, which],
        )

    small = [
        pltpu.make_async_copy(source, target, small_sem.at[i])
        for i, (source, target) in enumerate(
            ((sf_hbm, sf_ref), (skip_hbm, skip_ref), (gain_hbm, gain_ref), (mr_hbm, mr_ref))
        )
    ]
    for copy in small:
        copy.start()
    for step in range(n):
        dest = lax.rem(me + offset(step), n)
        for which in (1, 2, 0):
            load(dest, which).start()
    for k in range(1, n):
        pl.semaphore_signal(barrier, inc=1, device_id={"ctx": lax.rem(me + k, n)})
    for k in range(1, nz):
        pl.semaphore_signal(barrier, inc=1, device_id={"ch": lax.rem(mz + k, nz)})

    positions = me * rows_here + lax.broadcasted_iota(jnp.int32, (1, rows_here), 1)
    starts = jnp.zeros((1, rows_here), jnp.int32)
    first = jnp.int32(0)
    for d in range(docs_ref.shape[0]):
        starts = jnp.where(positions >= first, first, starts)
        first = first + docs_ref[d]
    for lag in (1, 2):
        lagmask[lag : lag + 1, :] = jnp.where(positions - lag >= starts, 1.0, 0.0).astype(F32)
    for copy in small:
        copy.wait()

    def make_masks():
        s_index = lax.broadcasted_iota(jnp.int32, (LANES, LANES), 0)
        t_index = lax.broadcasted_iota(jnp.int32, (LANES, LANES), 1)
        for tile in range(tiles):
            start_row = starts[:, tile * LANES : (tile + 1) * LANES]
            here = me * rows_here + tile * LANES + s_index
            before = (t_index < s_index) & (here - LANES >= start_row)
            within = (t_index >= s_index) & (here >= start_row)
            masks[tile, 0:LANES, :] = jnp.where(before, 1.0, 0.0).astype(BF16)
            masks[tile, LANES : 2 * LANES, :] = jnp.where(within, 1.0, 0.0).astype(BF16)

    def coefficients(first):
        span = pl.ds(pl.multiple_of(first, LANES), LANES)
        parts = [sf_ref[a, :, span] for a in range(3)] + [skip_ref[:, span], gain_ref[:, span]]
        parts.append(jnp.zeros((5, LANES), F32))
        coef[span, 0:16] = jnp.concatenate(parts, axis=0).T

    by_chunk = chunk % LANES == 0
    if not by_chunk:
        for b in range(channels // LANES):
            coefficients(b * LANES)

    row16 = lax.broadcasted_iota(jnp.int32, (16, LANES), 0)
    lane16 = lax.broadcasted_iota(jnp.int32, (16, LANES), 1)

    def pick(which):
        hit = (lane16 - (LANES - 2) == row16 - 2 * which) & (lane16 >= LANES - 2)
        return jnp.where(hit, 1.0, 0.0).astype(BF16)

    last = tiles * LANES

    right = lax.rem(me + 1, n)

    def chunk_rows(c):
        return pl.ds(pl.multiple_of(c * chunk, chunk), chunk)

    def raw_copy(c):
        return pltpu.make_async_remote_copy(
            src_ref=raw_send.at[c],
            dst_ref=raw_recv.at[c],
            send_sem=halo_send.at[c, 0],
            recv_sem=halo_recv.at[c, 0],
            device_id={"ctx": right},
        )

    def product_copy(c):
        return pltpu.make_async_remote_copy(
            src_ref=halo_out.at[chunk_rows(c)],
            dst_ref=halo_in.at[chunk_rows(c)],
            send_sem=halo_send.at[c, 1],
            recv_sem=halo_recv.at[c, 1],
            device_id={"ctx": right},
        )

    @pl.when(me == 0)
    def _():
        raw_recv[...] = jnp.zeros(raw_recv.shape, BF16)
        halo_in[...] = jnp.zeros(halo_in.shape, BF16)

    def take_raw(c):
        columns = jnp.zeros((16, chunk), F32)
        for which, ref in enumerate((g_ext, k_ext, v_ext)):
            columns = columns + lax.dot_general(
                pick(which),
                ref[chunk_rows(c), last : last + LANES],
                (((1,), (1,)), ((), ())),
                preferred_element_type=F32,
            )
        raw_send[c] = columns.astype(BF16)

    def spread_raw(c):
        for which, ref in enumerate((g_ext, k_ext, v_ext)):
            ref[chunk_rows(c), 0:LANES] = lax.dot_general(
                raw_recv[c],
                pick(which),
                (((0,), (0,)), ((), ())),
                preferred_element_type=F32,
            ).astype(BF16)

    def build(g):
        taps = jnp.broadcast_to(mr_ref[pl.ds(g, 1), :], (LANES, LANES))
        circ[g] = pltpu.roll(taps, 0, 1, stride=1, stride_axis=0).astype(BF16)

    def products(g, first_tile, count):
        rows = pl.ds(pl.multiple_of(g * GROUP, GROUP), GROUP)
        lanes = slice(first_tile * LANES, (first_tile + count) * LANES)
        m1, m2 = lagmask[1:2, lanes], lagmask[2:3, lanes]
        kc = short_conv(k_ext, coef, rows, first_tile, count, 1, m1, m2)
        vc = short_conv(v_ext, coef, rows, first_tile, count, 2, m1, m2)
        result = (kc * vc).astype(BF16)
        p_ext[rows, (first_tile + 1) * LANES : (first_tile + 1 + count) * LANES] = result
        if first_tile + count == tiles:
            halo_out[rows] = result[:, (count - 1) * LANES :]

    acc[...] = jnp.zeros(acc.shape, F32)

    def mix(g, first_tile, count):
        rows = pl.ds(pl.multiple_of(g * GROUP, 2 * GROUP), 2 * GROUP)
        lanes = slice(first_tile * LANES, (first_tile + count) * LANES)
        both = jnp.concatenate([circ[g], circ[g + 1]], axis=1)
        pair = jnp.concatenate([both, both], axis=0)
        parts = []
        for tile in range(first_tile, first_tile + count):
            mask = masks[tile]
            if tile == 0:
                window = jnp.concatenate([halo_in[rows], p_ext[rows, LANES : 2 * LANES]], axis=1)
            else:
                window = p_ext[rows, tile * LANES : (tile + 2) * LANES]
            result = jnp.dot(
                window,
                pair * jnp.concatenate([mask, mask], axis=1),
                preferred_element_type=F32,
            )
            parts.append(
                jnp.concatenate([result[:GROUP, :LANES], result[GROUP:, LANES:]], axis=0)
            )
        mixed = parts[0] if count == 1 else jnp.concatenate(parts, axis=1)
        direct = p_ext[rows, (first_tile + 1) * LANES : (first_tile + 1 + count) * LANES]
        mixed = mixed + coef[rows, 9:10] * direct.astype(F32)
        gate = short_conv(
            g_ext, coef, rows, first_tile, count, 0, lagmask[1:2, lanes], lagmask[2:3, lanes]
        )
        gated = gate * mixed
        sendbuf[0 if first_tile else 1, rows] = (gated * coef[rows, 10:11]).astype(BF16)
        squares = gated * gated
        return squares[0:8] + squares[8:16] + squares[16:24] + squares[24:32]

    def data_copy(dest, source, half):
        return pltpu.make_async_remote_copy(
            src_ref=sendbuf.at[half, chunk_rows(dest)],
            dst_ref=recv_ref.at[source, half],
            send_sem=data_send.at[dest, half],
            recv_sem=data_recv.at[source, half],
            device_id={"ctx": dest},
        )

    def own_copy(half):
        return pltpu.make_async_copy(
            sendbuf.at[half, chunk_rows(me)], recv_ref.at[me, half], data_send.at[me, half]
        )

    def stage(half, first_tile, count):
        lanes = slice(first_tile * LANES, (first_tile + count) * LANES)
        together = min(16, chunk_groups)
        unroll = min(8, chunk_groups)

        def one(step, carry):
            k = offset(step)
            dest = lax.rem(me + k, n)
            first_group = dest * chunk_groups
            if half == 0:
                if by_chunk:
                    for b in range(chunk // LANES):
                        coefficients(dest * chunk + b * LANES)
                load(dest, 1).wait()
                load(dest, 2).wait()

                def early(i, c):
                    build(first_group + i)
                    products(first_group + i, 1, tiles - 1)
                    return c

                lax.fori_loop(0, chunk_groups, early, 0, unroll=unroll)
                load(dest, 0).wait()
                take_raw(dest)

                @pl.when(step == 0)
                def _():
                    pl.semaphore_wait(barrier, n - 1 + nz - 1)

                @pl.when(me < n - 1)
                def _():
                    raw_copy(dest).start()
                    product_copy(dest).start()

                @pl.when(step == 0)
                def _():
                    make_masks()

            else:

                @pl.when(me > 0)
                def _():
                    raw_copy(dest).wait_recv()
                    product_copy(dest).wait_recv()

                spread_raw(dest)

                def rest(i, c):
                    products(first_group + i, 0, 1)
                    return c

                lax.fori_loop(0, chunk_groups, rest, 0, unroll=unroll)

            def some(i, c):
                total = jnp.zeros((8, count * LANES), F32)
                for j in range(0, together, 2):
                    total = total + mix(first_group + i * together + j, first_tile, count)
                acc[:, lanes] += total
                return c

            lax.fori_loop(0, chunk_groups // together, some, 0)

            @pl.when(k != 0)
            def _():
                data_copy(dest, me, half).start()

            @pl.when(k == 0)
            def _():
                own_copy(half).start()

            return carry

        lax.fori_loop(0, n, one, 0)

    stage(0, tiles // 2, tiles - tiles // 2)
    stage(1, 0, tiles // 2)

    sq_all[mz] = jnp.sum(acc[...], axis=0, keepdims=True)

    def sq_copy(dest, source):
        return pltpu.make_async_remote_copy(
            src_ref=sq_all.at[mz],
            dst_ref=sq_all.at[source],
            send_sem=sq_send.at[dest],
            recv_sem=sq_recv.at[source],
            device_id={"ch": dest},
        )

    for k in range(1, nz):
        sq_copy(lax.rem(mz + k, nz), mz).start()
    for k in range(1, nz):
        sq_copy(mz, lax.rem(mz + k, nz)).wait_recv()
    total = sq_all[0]
    for z in range(1, nz):
        total = total + sq_all[z]
    own_scale[0] = lax.rsqrt(total / D + NORM_EPS)
    keep_scale = pltpu.make_async_copy(own_scale.at[0], scale_ref.at[me], sc_send.at[me])
    keep_scale.start()

    def sc_copy(dest, source):
        return pltpu.make_async_remote_copy(
            src_ref=own_scale.at[0],
            dst_ref=scale_ref.at[source],
            send_sem=sc_send.at[dest],
            recv_sem=sc_recv.at[source],
            device_id={"ctx": dest},
        )

    for k in range(1, n):
        sc_copy(lax.rem(me + k, n), me).start()
    for k in range(1, n):
        sc_copy(me, lax.rem(me + k, n)).wait_recv()
    keep_scale.wait()

    def finish(k, carry):
        other = lax.rem(me + k, n)
        for half in (0, 1):
            data_copy(me, other, half).wait_recv()
            data_copy(other, me, half).wait_send()
        sc_copy(other, me).wait_send()
        return carry

    lax.fori_loop(1, n, finish, 0)
    own_copy(0).wait()
    own_copy(1).wait()
    for k in range(1, nz):
        sq_copy(lax.rem(mz + k, nz), mz).wait_send()

    @pl.when(me < n - 1)
    def _():
        def sent(c, carry):
            raw_copy(c).wait_send()
            product_copy(c).wait_send()
            return carry

        lax.fori_loop(0, n, sent, 0)


def scale_kernel(source, scales_hbm, target, held, scaled, scales, scale_sem, load_sem, store_sem):
    n, _, _, width = source.shape
    fetch = pltpu.make_async_copy(scales_hbm, scales, scale_sem)
    fetch.start()
    loads, stores = [], []
    for i in range(n):
        lanes = slice(2 * i * width, 2 * (i + 1) * width)
        loads.append(pltpu.make_async_copy(source.at[i], held.at[i], load_sem.at[i]))
        stores.append(pltpu.make_async_copy(scaled.at[:, lanes], target.at[:, lanes], store_sem.at[i]))
        loads[i].start()
    fetch.wait()
    for i in range(n):
        loads[i].wait()
        for half in range(2):
            first = (2 * i + 1 - half) * width
            scale = scales[i, :, (1 - half) * width : (2 - half) * width]
            scaled[:, first : first + width] = (held[i, half].astype(F32) * scale).astype(BF16)
        stores[i].start()
    for store in stores:
        store.wait()


def local(
    n, nz, gate_input, key_input, value_input, short_filter, mr_filter, mr_skip, norm_gain, doc_lengths
):
    channels, rows_here = gate_input.shape
    chunk = channels // n
    groups = channels // GROUP
    tiles = rows_here // LANES
    ext = pltpu.VMEM((channels, rows_here + LANES), BF16)
    anywhere = pl.BlockSpec(memory_space=pl.ANY)
    hbm = pl.BlockSpec(memory_space=pltpu.HBM)
    dma = pltpu.SemaphoreType.DMA
    received, scales = pl.pallas_call(
        functools.partial(kernel, n, nz),
        out_shape=(
            jax.ShapeDtypeStruct((n, 2, chunk, rows_here // 2), BF16),
            jax.ShapeDtypeStruct((n, 1, rows_here), F32),
        ),
        in_specs=[hbm] * 7 + [pl.BlockSpec(memory_space=pltpu.SMEM)],
        out_specs=(anywhere, anywhere),
        scratch_shapes=[
            ext,
            ext,
            ext,
            ext,
            pltpu.VMEM((groups, LANES, LANES), BF16),
            pltpu.VMEM((channels, LANES), F32),
            pltpu.VMEM((tiles, 2 * LANES, LANES), BF16),
            pltpu.VMEM((8, rows_here), F32),
            pltpu.VMEM((2, channels, rows_here // 2), BF16),
            pltpu.VMEM((n, 16, chunk), BF16),
            pltpu.VMEM((n, 16, chunk), BF16),
            pltpu.VMEM((channels, LANES), BF16),
            pltpu.VMEM((channels, LANES), BF16),
            pltpu.VMEM((8, rows_here), F32),
            pltpu.VMEM((nz, 1, rows_here), F32),
            pltpu.VMEM((1, 1, rows_here), F32),
            pltpu.VMEM((3, SHORT, channels), F32),
            pltpu.VMEM((groups, MR), F32),
            pltpu.VMEM((1, channels), F32),
            pltpu.VMEM((1, channels), F32),
            dma((4,)),
            dma((n, 3)),
            dma((n, 2)),
            dma((n, 2)),
            dma((n, 2)),
            dma((n, 2)),
            dma((nz,)),
            dma((nz,)),
            dma((n,)),
            dma((n,)),
        ],
        compiler_params=pltpu.CompilerParams(
            collective_id=0, has_side_effects=True, vmem_limit_bytes=56 * 1024 * 1024
        ),
        cost_estimate=pl.CostEstimate(
            flops=channels * rows_here * 600, bytes_accessed=channels * rows_here * 8, transcendentals=0
        ),
    )(
        gate_input,
        key_input,
        value_input,
        short_filter,
        mr_filter,
        mr_skip.reshape(1, channels),
        norm_gain.reshape(1, channels),
        doc_lengths,
    )
    return pl.pallas_call(
        scale_kernel,
        out_shape=jax.ShapeDtypeStruct((chunk, n * rows_here), BF16),
        in_specs=[anywhere, anywhere],
        out_specs=anywhere,
        scratch_shapes=[
            pltpu.VMEM(received.shape, BF16),
            pltpu.VMEM((chunk, n * rows_here), BF16),
            pltpu.VMEM(scales.shape, F32),
            dma(()),
            dma((n,)),
            dma((n,)),
        ],
        compiler_params=pltpu.CompilerParams(vmem_limit_bytes=56 * 1024 * 1024),
    )(received, scales)


def solution(mesh):
    n, nz = mesh.shape["ctx"], mesh.shape["ch"]
    in_specs = (
        P("ch", "ctx"),
        P("ch", "ctx"),
        P("ch", "ctx"),
        P(None, None, "ch"),
        P("ch", None),
        P("ch"),
        P("ch"),
        P(),
    )
    out_specs = P(("ch", "ctx"), None)
    return jax.shard_map(
        functools.partial(local, n, nz), mesh=mesh, in_specs=in_specs, out_specs=out_specs, check_vma=False
    )
```

```python
import functools

import jax
import jax.numpy as jnp
from jax import lax
from jax.experimental import pallas as pl
from jax.experimental.pallas import tpu as pltpu
from jax.sharding import PartitionSpec as P

D = 8192
GROUP = 16
SHORT = 3
MR = 128
NORM_EPS = 1e-06

LANES = 128
F32 = jnp.float32
BF16 = jnp.bfloat16


def short_conv(ext_ref, coef_ref, rows, first_tile, tiles, which, m1, m2):
    width = (tiles + 1) * LANES
    x = ext_ref[rows, first_tile * LANES : first_tile * LANES + width].astype(F32)
    x1 = pltpu.roll(x, 1, 1)[:, LANES:]
    x2 = pltpu.roll(x, 2, 1)[:, LANES:]
    base = which * SHORT
    c0 = coef_ref[rows, base : base + 1]
    c1 = coef_ref[rows, base + 1 : base + 2]
    c2 = coef_ref[rows, base + 2 : base + 3]
    return c0 * x[:, LANES:] + c1 * (x1 * m1) + c2 * (x2 * m2)


def kernel(
    n,
    nz,
    gate_hbm,
    key_hbm,
    value_hbm,
    sf_hbm,
    mr_hbm,
    skip_hbm,
    gain_hbm,
    docs_ref,
    recv_ref,
    scale_ref,
    g_ext,
    k_ext,
    v_ext,
    p_ext,
    circ,
    coef,
    masks,
    lagmask,
    sendbuf,
    raw_send,
    raw_recv,
    halo_out,
    halo_in,
    acc,
    sq_all,
    own_scale,
    sf_ref,
    mr_ref,
    skip_ref,
    gain_ref,
    small_sem,
    load_sem,
    halo_send,
    halo_recv,
    data_send,
    data_recv,
    sq_send,
    sq_recv,
    sc_send,
    sc_recv,
):
    me = lax.axis_index("ctx")
    mz = lax.axis_index("ch")
    channels, rows_here = gate_hbm.shape
    chunk = channels // n
    groups = channels // GROUP
    tiles = rows_here // LANES
    chunk_groups = chunk // GROUP
    barrier = pltpu.get_barrier_semaphore()

    def offset(step):
        odd = (step + n // 2 + 1) // n
        return ((2 * (step + 1) + 3 * odd) % n) * (1 - (step + 1) // n)

    def load(b, which):
        source = (gate_hbm, key_hbm, value_hbm)[which]
        target = (g_ext, k_ext, v_ext)[which]
        span = pl.ds(pl.multiple_of(b * chunk, chunk), chunk)
        return pltpu.make_async_copy(
            source.at[span, :],
            target.at[span, LANES : LANES + rows_here],
            load_sem.at[b, which],
        )

    small = [
        pltpu.make_async_copy(source, target, small_sem.at[i])
        for i, (source, target) in enumerate(
            ((sf_hbm, sf_ref), (skip_hbm, skip_ref), (gain_hbm, gain_ref), (mr_hbm, mr_ref))
        )
    ]
    for copy in small:
        copy.start()
    for step in range(n):
        dest = lax.rem(me + offset(step), n)
        for which in (1, 2, 0):
            load(dest, which).start()
    for k in range(1, n):
        pl.semaphore_signal(barrier, inc=1, device_id={"ctx": lax.rem(me + k, n)})
    for k in range(1, nz):
        pl.semaphore_signal(barrier, inc=1, device_id={"ch": lax.rem(mz + k, nz)})

    positions = me * rows_here + lax.broadcasted_iota(jnp.int32, (1, rows_here), 1)
    starts = jnp.zeros((1, rows_here), jnp.int32)
    first = jnp.int32(0)
    for d in range(docs_ref.shape[0]):
        starts = jnp.where(positions >= first, first, starts)
        first = first + docs_ref[d]
    for lag in (1, 2):
        lagmask[lag : lag + 1, :] = jnp.where(positions - lag >= starts, 1.0, 0.0).astype(F32)
    for copy in small:
        copy.wait()

    def make_masks():
        s_index = lax.broadcasted_iota(jnp.int32, (LANES, LANES), 0)
        t_index = lax.broadcasted_iota(jnp.int32, (LANES, LANES), 1)
        for tile in range(tiles):
            start_row = starts[:, tile * LANES : (tile + 1) * LANES]
            here = me * rows_here + tile * LANES + s_index
            before = (t_index < s_index) & (here - LANES >= start_row)
            within = (t_index >= s_index) & (here >= start_row)
            masks[tile, 0:LANES, :] = jnp.where(before, 1.0, 0.0).astype(BF16)
            masks[tile, LANES : 2 * LANES, :] = jnp.where(within, 1.0, 0.0).astype(BF16)

    def coefficients(first):
        span = pl.ds(pl.multiple_of(first, LANES), LANES)
        parts = [sf_ref[a, :, span] for a in range(3)] + [skip_ref[:, span], gain_ref[:, span]]
        parts.append(jnp.zeros((5, LANES), F32))
        coef[span, 0:16] = jnp.concatenate(parts, axis=0).T

    by_chunk = chunk % LANES == 0
    if not by_chunk:
        for b in range(channels // LANES):
            coefficients(b * LANES)

    row16 = lax.broadcasted_iota(jnp.int32, (16, LANES), 0)
    lane16 = lax.broadcasted_iota(jnp.int32, (16, LANES), 1)

    def pick(which):
        hit = (lane16 - (LANES - 2) == row16 - 2 * which) & (lane16 >= LANES - 2)
        return jnp.where(hit, 1.0, 0.0).astype(BF16)

    last = tiles * LANES

    right = lax.rem(me + 1, n)

    def chunk_rows(c):
        return pl.ds(pl.multiple_of(c * chunk, chunk), chunk)

    def raw_copy(c):
        return pltpu.make_async_remote_copy(
            src_ref=raw_send.at[c],
            dst_ref=raw_recv.at[c],
            send_sem=halo_send.at[c, 0],
            recv_sem=halo_recv.at[c, 0],
            device_id={"ctx": right},
        )

    def product_copy(c):
        return pltpu.make_async_remote_copy(
            src_ref=halo_out.at[chunk_rows(c)],
            dst_ref=halo_in.at[chunk_rows(c)],
            send_sem=halo_send.at[c, 1],
            recv_sem=halo_recv.at[c, 1],
            device_id={"ctx": right},
        )

    @pl.when(me == 0)
    def _():
        raw_recv[...] = jnp.zeros(raw_recv.shape, BF16)
        halo_in[...] = jnp.zeros(halo_in.shape, BF16)

    def take_raw(c):
        columns = jnp.zeros((16, chunk), F32)
        for which, ref in enumerate((g_ext, k_ext, v_ext)):
            columns = columns + lax.dot_general(
                pick(which),
                ref[chunk_rows(c), last : last + LANES],
                (((1,), (1,)), ((), ())),
                preferred_element_type=F32,
            )
        raw_send[c] = columns.astype(BF16)

    def spread_raw(c):
        for which, ref in enumerate((g_ext, k_ext, v_ext)):
            ref[chunk_rows(c), 0:LANES] = lax.dot_general(
                raw_recv[c],
                pick(which),
                (((0,), (0,)), ((), ())),
                preferred_element_type=F32,
            ).astype(BF16)

    def build(g):
        taps = jnp.broadcast_to(mr_ref[pl.ds(g, 1), :], (LANES, LANES))
        circ[g] = pltpu.roll(taps, 0, 1, stride=1, stride_axis=0).astype(BF16)

    def products(g, first_tile, count):
        rows = pl.ds(pl.multiple_of(g * GROUP, GROUP), GROUP)
        lanes = slice(first_tile * LANES, (first_tile + count) * LANES)
        m1, m2 = lagmask[1:2, lanes], lagmask[2:3, lanes]
        kc = short_conv(k_ext, coef, rows, first_tile, count, 1, m1, m2)
        vc = short_conv(v_ext, coef, rows, first_tile, count, 2, m1, m2)
        result = (kc * vc).astype(BF16)
        p_ext[rows, (first_tile + 1) * LANES : (first_tile + 1 + count) * LANES] = result
        if first_tile + count == tiles:
            halo_out[rows] = result[:, (count - 1) * LANES :]

    acc[...] = jnp.zeros(acc.shape, F32)

    def mix(g, first_tile, count):
        rows = pl.ds(pl.multiple_of(g * GROUP, 2 * GROUP), 2 * GROUP)
        lanes = slice(first_tile * LANES, (first_tile + count) * LANES)
        both = jnp.concatenate([circ[g], circ[g + 1]], axis=1)
        pair = jnp.concatenate([both, both], axis=0)
        parts = []
        for tile in range(first_tile, first_tile + count):
            mask = masks[tile]
            if tile == 0:
                window = jnp.concatenate([halo_in[rows], p_ext[rows, LANES : 2 * LANES]], axis=1)
            else:
                window = p_ext[rows, tile * LANES : (tile + 2) * LANES]
            result = jnp.dot(
                window,
                pair * jnp.concatenate([mask, mask], axis=1),
                preferred_element_type=F32,
            )
            parts.append(
                jnp.concatenate([result[:GROUP, :LANES], result[GROUP:, LANES:]], axis=0)
            )
        mixed = parts[0] if count == 1 else jnp.concatenate(parts, axis=1)
        direct = p_ext[rows, (first_tile + 1) * LANES : (first_tile + 1 + count) * LANES]
        mixed = mixed + coef[rows, 9:10] * direct.astype(F32)
        gate = short_conv(
            g_ext, coef, rows, first_tile, count, 0, lagmask[1:2, lanes], lagmask[2:3, lanes]
        )
        gated = gate * mixed
        sendbuf[0 if first_tile else 1, rows] = (gated * coef[rows, 10:11]).astype(BF16)
        squares = gated * gated
        return squares[0:8] + squares[8:16] + squares[16:24] + squares[24:32]

    def data_copy(dest, source, half):
        return pltpu.make_async_remote_copy(
            src_ref=sendbuf.at[half, chunk_rows(dest)],
            dst_ref=recv_ref.at[source, half],
            send_sem=data_send.at[dest, half],
            recv_sem=data_recv.at[source, half],
            device_id={"ctx": dest},
        )

    def own_copy(half):
        return pltpu.make_async_copy(
            sendbuf.at[half, chunk_rows(me)], recv_ref.at[me, half], data_send.at[me, half]
        )

    def stage(half, first_tile, count):
        lanes = slice(first_tile * LANES, (first_tile + count) * LANES)
        together = min(16, chunk_groups)
        unroll = min(8, chunk_groups)

        def one(step, carry):
            k = offset(step)
            dest = lax.rem(me + k, n)
            first_group = dest * chunk_groups
            if half == 0:
                if by_chunk:
                    for b in range(chunk // LANES):
                        coefficients(dest * chunk + b * LANES)
                load(dest, 1).wait()
                load(dest, 2).wait()

                def early(i, c):
                    build(first_group + i)
                    products(first_group + i, 1, tiles - 1)
                    return c

                lax.fori_loop(0, chunk_groups, early, 0, unroll=unroll)
                load(dest, 0).wait()
                take_raw(dest)

                @pl.when(step == 1)
                def _():
                    pl.semaphore_wait(barrier, n - 1 + nz - 1)
                    held = lax.rem(me + offset(0), n)

                    @pl.when(me < n - 1)
                    def _():
                        raw_copy(held).start()
                        product_copy(held).start()

                    data_copy(held, me, 0).start()

                @pl.when((step > 0) & (me < n - 1))
                def _():
                    raw_copy(dest).start()
                    product_copy(dest).start()

                @pl.when(step == 0)
                def _():
                    make_masks()

            else:

                @pl.when(me > 0)
                def _():
                    raw_copy(dest).wait_recv()
                    product_copy(dest).wait_recv()

                spread_raw(dest)

                def rest(i, c):
                    products(first_group + i, 0, 1)
                    return c

                lax.fori_loop(0, chunk_groups, rest, 0, unroll=unroll)

            def some(i, c):
                total = jnp.zeros((8, count * LANES), F32)
                for j in range(0, together, 2):
                    total = total + mix(first_group + i * together + j, first_tile, count)
                acc[:, lanes] += total
                return c

            lax.fori_loop(0, chunk_groups // together, some, 0)

            @pl.when((k != 0) & ((step > 0) | (half == 1)))
            def _():
                data_copy(dest, me, half).start()

            @pl.when(k == 0)
            def _():
                own_copy(half).start()

            return carry

        lax.fori_loop(0, n, one, 0)

    stage(0, tiles // 2, tiles - tiles // 2)
    stage(1, 0, tiles // 2)

    sq_all[mz] = jnp.sum(acc[...], axis=0, keepdims=True)

    def sq_copy(dest, source):
        return pltpu.make_async_remote_copy(
            src_ref=sq_all.at[mz],
            dst_ref=sq_all.at[source],
            send_sem=sq_send.at[dest],
            recv_sem=sq_recv.at[source],
            device_id={"ch": dest},
        )

    for k in range(1, nz):
        sq_copy(lax.rem(mz + k, nz), mz).start()
    for k in range(1, nz):
        sq_copy(mz, lax.rem(mz + k, nz)).wait_recv()
    total = sq_all[0]
    for z in range(1, nz):
        total = total + sq_all[z]
    own_scale[0] = lax.rsqrt(total / D + NORM_EPS)
    keep_scale = pltpu.make_async_copy(own_scale.at[0], scale_ref.at[me], sc_send.at[me])
    keep_scale.start()

    def sc_copy(dest, source):
        return pltpu.make_async_remote_copy(
            src_ref=own_scale.at[0],
            dst_ref=scale_ref.at[source],
            send_sem=sc_send.at[dest],
            recv_sem=sc_recv.at[source],
            device_id={"ctx": dest},
        )

    for k in range(1, n):
        sc_copy(lax.rem(me + k, n), me).start()
    for k in range(1, n):
        sc_copy(me, lax.rem(me + k, n)).wait_recv()
    keep_scale.wait()

    def finish(k, carry):
        other = lax.rem(me + k, n)
        for half in (0, 1):
            data_copy(me, other, half).wait_recv()
            data_copy(other, me, half).wait_send()
        sc_copy(other, me).wait_send()
        return carry

    lax.fori_loop(1, n, finish, 0)
    own_copy(0).wait()
    own_copy(1).wait()
    for k in range(1, nz):
        sq_copy(lax.rem(mz + k, nz), mz).wait_send()

    @pl.when(me < n - 1)
    def _():
        def sent(c, carry):
            raw_copy(c).wait_send()
            product_copy(c).wait_send()
            return carry

        lax.fori_loop(0, n, sent, 0)


def scale_kernel(source, scales_hbm, target, held, scaled, scales, scale_sem, load_sem, store_sem):
    n, _, _, width = source.shape
    fetch = pltpu.make_async_copy(scales_hbm, scales, scale_sem)
    fetch.start()
    loads, stores = [], []
    for i in range(n):
        lanes = slice(2 * i * width, 2 * (i + 1) * width)
        loads.append(pltpu.make_async_copy(source.at[i], held.at[i], load_sem.at[i]))
        stores.append(pltpu.make_async_copy(scaled.at[:, lanes], target.at[:, lanes], store_sem.at[i]))
        loads[i].start()
    fetch.wait()
    for i in range(n):
        loads[i].wait()
        for half in range(2):
            first = (2 * i + 1 - half) * width
            scale = scales[i, :, (1 - half) * width : (2 - half) * width]
            scaled[:, first : first + width] = (held[i, half].astype(F32) * scale).astype(BF16)
        stores[i].start()
    for store in stores:
        store.wait()


def local(
    n, nz, gate_input, key_input, value_input, short_filter, mr_filter, mr_skip, norm_gain, doc_lengths
):
    channels, rows_here = gate_input.shape
    chunk = channels // n
    groups = channels // GROUP
    tiles = rows_here // LANES
    ext = pltpu.VMEM((channels, rows_here + LANES), BF16)
    anywhere = pl.BlockSpec(memory_space=pl.ANY)
    hbm = pl.BlockSpec(memory_space=pltpu.HBM)
    dma = pltpu.SemaphoreType.DMA
    received, scales = pl.pallas_call(
        functools.partial(kernel, n, nz),
        out_shape=(
            jax.ShapeDtypeStruct((n, 2, chunk, rows_here // 2), BF16),
            jax.ShapeDtypeStruct((n, 1, rows_here), F32),
        ),
        in_specs=[hbm] * 7 + [pl.BlockSpec(memory_space=pltpu.SMEM)],
        out_specs=(anywhere, anywhere),
        scratch_shapes=[
            ext,
            ext,
            ext,
            ext,
            pltpu.VMEM((groups, LANES, LANES), BF16),
            pltpu.VMEM((channels, LANES), F32),
            pltpu.VMEM((tiles, 2 * LANES, LANES), BF16),
            pltpu.VMEM((8, rows_here), F32),
            pltpu.VMEM((2, channels, rows_here // 2), BF16),
            pltpu.VMEM((n, 16, chunk), BF16),
            pltpu.VMEM((n, 16, chunk), BF16),
            pltpu.VMEM((channels, LANES), BF16),
            pltpu.VMEM((channels, LANES), BF16),
            pltpu.VMEM((8, rows_here), F32),
            pltpu.VMEM((nz, 1, rows_here), F32),
            pltpu.VMEM((1, 1, rows_here), F32),
            pltpu.VMEM((3, SHORT, channels), F32),
            pltpu.VMEM((groups, MR), F32),
            pltpu.VMEM((1, channels), F32),
            pltpu.VMEM((1, channels), F32),
            dma((4,)),
            dma((n, 3)),
            dma((n, 2)),
            dma((n, 2)),
            dma((n, 2)),
            dma((n, 2)),
            dma((nz,)),
            dma((nz,)),
            dma((n,)),
            dma((n,)),
        ],
        compiler_params=pltpu.CompilerParams(
            collective_id=0, has_side_effects=True, vmem_limit_bytes=56 * 1024 * 1024
        ),
        cost_estimate=pl.CostEstimate(
            flops=channels * rows_here * 600, bytes_accessed=channels * rows_here * 8, transcendentals=0
        ),
    )(
        gate_input,
        key_input,
        value_input,
        short_filter,
        mr_filter,
        mr_skip.reshape(1, channels),
        norm_gain.reshape(1, channels),
        doc_lengths,
    )
    return pl.pallas_call(
        scale_kernel,
        out_shape=jax.ShapeDtypeStruct((chunk, n * rows_here), BF16),
        in_specs=[anywhere, anywhere],
        out_specs=anywhere,
        scratch_shapes=[
            pltpu.VMEM(received.shape, BF16),
            pltpu.VMEM((chunk, n * rows_here), BF16),
            pltpu.VMEM(scales.shape, F32),
            dma(()),
            dma((n,)),
            dma((n,)),
        ],
        compiler_params=pltpu.CompilerParams(vmem_limit_bytes=56 * 1024 * 1024),
    )(received, scales)


def solution(mesh):
    n, nz = mesh.shape["ctx"], mesh.shape["ch"]
    in_specs = (
        P("ch", "ctx"),
        P("ch", "ctx"),
        P("ch", "ctx"),
        P(None, None, "ch"),
        P("ch", None),
        P("ch"),
        P("ch"),
        P(),
    )
    out_specs = P(("ch", "ctx"), None)
    return jax.shard_map(
        functools.partial(local, n, nz), mesh=mesh, in_specs=in_specs, out_specs=out_specs, check_vma=False
    )
```

```python
import functools

import jax
import jax.numpy as jnp
from jax import lax
from jax.experimental import pallas as pl
from jax.experimental.pallas import tpu as pltpu
from jax.sharding import PartitionSpec as P

D = 8192
GROUP = 16
SHORT = 3
MR = 128
NORM_EPS = 1e-06

LANES = 128
F32 = jnp.float32
BF16 = jnp.bfloat16


def short_conv(ext_ref, coef_ref, rows, first_tile, tiles, which, m1, m2):
    width = (tiles + 1) * LANES
    x = ext_ref[rows, first_tile * LANES : first_tile * LANES + width].astype(F32)
    x1 = pltpu.roll(x, 1, 1)[:, LANES:]
    x2 = pltpu.roll(x, 2, 1)[:, LANES:]
    base = which * SHORT
    c0 = coef_ref[rows, base : base + 1]
    c1 = coef_ref[rows, base + 1 : base + 2]
    c2 = coef_ref[rows, base + 2 : base + 3]
    return c0 * x[:, LANES:] + c1 * (x1 * m1) + c2 * (x2 * m2)


def kernel(
    n,
    nz,
    gate_hbm,
    key_hbm,
    value_hbm,
    sf_hbm,
    mr_hbm,
    skip_hbm,
    gain_hbm,
    docs_ref,
    recv_ref,
    scale_ref,
    g_ext,
    k_ext,
    v_ext,
    p_ext,
    circ,
    coef,
    masks,
    lagmask,
    sendbuf,
    raw_send,
    raw_recv,
    halo_out,
    halo_in,
    acc,
    sq_all,
    own_scale,
    sf_ref,
    mr_ref,
    skip_ref,
    gain_ref,
    small_sem,
    load_sem,
    halo_send,
    halo_recv,
    data_send,
    data_recv,
    sq_send,
    sq_recv,
    sc_send,
    sc_recv,
):
    me = lax.axis_index("ctx")
    mz = lax.axis_index("ch")
    channels, rows_here = gate_hbm.shape
    chunk = channels // n
    groups = channels // GROUP
    tiles = rows_here // LANES
    chunk_groups = chunk // GROUP
    barrier = pltpu.get_barrier_semaphore()

    def offset(step):
        odd = (step + n // 2 + 1) // n
        return ((2 * (step + 1) + 3 * odd) % n) * (1 - (step + 1) // n)

    def load(b, which):
        source = (gate_hbm, key_hbm, value_hbm)[which]
        target = (g_ext, k_ext, v_ext)[which]
        span = pl.ds(pl.multiple_of(b * chunk, chunk), chunk)
        return pltpu.make_async_copy(
            source.at[span, :],
            target.at[span, LANES : LANES + rows_here],
            load_sem.at[b, which],
        )

    small = [
        pltpu.make_async_copy(source, target, small_sem.at[i])
        for i, (source, target) in enumerate(
            ((sf_hbm, sf_ref), (skip_hbm, skip_ref), (gain_hbm, gain_ref), (mr_hbm, mr_ref))
        )
    ]
    for copy in small:
        copy.start()
    for step in range(n):
        dest = lax.rem(me + offset(step), n)
        for which in (1, 2, 0):
            load(dest, which).start()
    for k in range(1, n):
        pl.semaphore_signal(barrier, inc=1, device_id={"ctx": lax.rem(me + k, n)})
    for k in range(1, nz):
        pl.semaphore_signal(barrier, inc=1, device_id={"ch": lax.rem(mz + k, nz)})

    positions = me * rows_here + lax.broadcasted_iota(jnp.int32, (1, rows_here), 1)
    starts = jnp.zeros((1, rows_here), jnp.int32)
    first = jnp.int32(0)
    for d in range(docs_ref.shape[0]):
        starts = jnp.where(positions >= first, first, starts)
        first = first + docs_ref[d]
    for lag in (1, 2):
        lagmask[lag : lag + 1, :] = jnp.where(positions - lag >= starts, 1.0, 0.0).astype(F32)
    for copy in small:
        copy.wait()

    def make_masks():
        s_index = lax.broadcasted_iota(jnp.int32, (LANES, LANES), 0)
        t_index = lax.broadcasted_iota(jnp.int32, (LANES, LANES), 1)
        for tile in range(tiles):
            start_row = starts[:, tile * LANES : (tile + 1) * LANES]
            here = me * rows_here + tile * LANES + s_index
            before = (t_index < s_index) & (here - LANES >= start_row)
            within = (t_index >= s_index) & (here >= start_row)
            masks[tile, 0:LANES, :] = jnp.where(before, 1.0, 0.0).astype(BF16)
            masks[tile, LANES : 2 * LANES, :] = jnp.where(within, 1.0, 0.0).astype(BF16)

    def coefficients(first):
        span = pl.ds(pl.multiple_of(first, LANES), LANES)
        parts = [sf_ref[a, :, span] for a in range(3)] + [skip_ref[:, span], gain_ref[:, span]]
        parts.append(jnp.zeros((5, LANES), F32))
        coef[span, 0:16] = jnp.concatenate(parts, axis=0).T

    by_chunk = chunk % LANES == 0
    if not by_chunk:
        for b in range(channels // LANES):
            coefficients(b * LANES)

    row16 = lax.broadcasted_iota(jnp.int32, (16, LANES), 0)
    lane16 = lax.broadcasted_iota(jnp.int32, (16, LANES), 1)

    def pick(which):
        hit = (lane16 - (LANES - 2) == row16 - 2 * which) & (lane16 >= LANES - 2)
        return jnp.where(hit, 1.0, 0.0).astype(BF16)

    last = tiles * LANES

    right = lax.rem(me + 1, n)

    def chunk_rows(c):
        return pl.ds(pl.multiple_of(c * chunk, chunk), chunk)

    def raw_copy(c):
        return pltpu.make_async_remote_copy(
            src_ref=raw_send.at[c],
            dst_ref=raw_recv.at[c],
            send_sem=halo_send.at[c, 0],
            recv_sem=halo_recv.at[c, 0],
            device_id={"ctx": right},
        )

    def product_copy(c):
        return pltpu.make_async_remote_copy(
            src_ref=halo_out.at[chunk_rows(c)],
            dst_ref=halo_in.at[chunk_rows(c)],
            send_sem=halo_send.at[c, 1],
            recv_sem=halo_recv.at[c, 1],
            device_id={"ctx": right},
        )

    @pl.when(me == 0)
    def _():
        raw_recv[...] = jnp.zeros(raw_recv.shape, BF16)
        halo_in[...] = jnp.zeros(halo_in.shape, BF16)

    def take_raw(c):
        columns = jnp.zeros((16, chunk), F32)
        for which, ref in enumerate((g_ext, k_ext, v_ext)):
            columns = columns + lax.dot_general(
                pick(which),
                ref[chunk_rows(c), last : last + LANES],
                (((1,), (1,)), ((), ())),
                preferred_element_type=F32,
            )
        raw_send[c] = columns.astype(BF16)

    def spread_raw(c):
        for which, ref in enumerate((g_ext, k_ext, v_ext)):
            ref[chunk_rows(c), 0:LANES] = lax.dot_general(
                raw_recv[c],
                pick(which),
                (((0,), (0,)), ((), ())),
                preferred_element_type=F32,
            ).astype(BF16)

    def build(g):
        taps = jnp.broadcast_to(mr_ref[pl.ds(g, 1), :], (LANES, LANES))
        circ[g] = pltpu.roll(taps, 0, 1, stride=1, stride_axis=0).astype(BF16)

    def products(g, first_tile, count):
        rows = pl.ds(pl.multiple_of(g * GROUP, GROUP), GROUP)
        lanes = slice(first_tile * LANES, (first_tile + count) * LANES)
        m1, m2 = lagmask[1:2, lanes], lagmask[2:3, lanes]
        kc = short_conv(k_ext, coef, rows, first_tile, count, 1, m1, m2)
        vc = short_conv(v_ext, coef, rows, first_tile, count, 2, m1, m2)
        result = (kc * vc).astype(BF16)
        p_ext[rows, (first_tile + 1) * LANES : (first_tile + 1 + count) * LANES] = result
        if first_tile + count == tiles:
            halo_out[rows] = result[:, (count - 1) * LANES :]

    acc[...] = jnp.zeros(acc.shape, F32)

    def mix(g, first_tile, count):
        rows = pl.ds(pl.multiple_of(g * GROUP, 2 * GROUP), 2 * GROUP)
        lanes = slice(first_tile * LANES, (first_tile + count) * LANES)
        both = jnp.concatenate([circ[g], circ[g + 1]], axis=1)
        pair = jnp.concatenate([both, both], axis=0)
        parts = []
        for tile in range(first_tile, first_tile + count):
            mask = masks[tile]
            if tile == 0:
                window = jnp.concatenate([halo_in[rows], p_ext[rows, LANES : 2 * LANES]], axis=1)
            else:
                window = p_ext[rows, tile * LANES : (tile + 2) * LANES]
            result = jnp.dot(
                window,
                pair * jnp.concatenate([mask, mask], axis=1),
                preferred_element_type=F32,
            )
            parts.append(
                jnp.concatenate([result[:GROUP, :LANES], result[GROUP:, LANES:]], axis=0)
            )
        mixed = parts[0] if count == 1 else jnp.concatenate(parts, axis=1)
        direct = p_ext[rows, (first_tile + 1) * LANES : (first_tile + 1 + count) * LANES]
        mixed = mixed + coef[rows, 9:10] * direct.astype(F32)
        gate = short_conv(
            g_ext, coef, rows, first_tile, count, 0, lagmask[1:2, lanes], lagmask[2:3, lanes]
        )
        gated = gate * mixed
        sendbuf[0 if first_tile else 1, rows] = (gated * coef[rows, 10:11]).astype(BF16)
        squares = gated * gated
        return squares[0:8] + squares[8:16] + squares[16:24] + squares[24:32]

    pieces = (2 if chunk_groups >= 16 else 1, 1)

    def data_copy(dest, source, half, piece):
        height = chunk // pieces[half]
        return pltpu.make_async_remote_copy(
            src_ref=sendbuf.at[
                half, pl.ds(pl.multiple_of(dest * chunk + piece * height, height), height)
            ],
            dst_ref=recv_ref.at[source, half, piece * height : (piece + 1) * height],
            send_sem=data_send.at[dest, half, piece],
            recv_sem=data_recv.at[source, half, piece],
            device_id={"ctx": dest},
        )

    def own_copy(half):
        return pltpu.make_async_copy(
            sendbuf.at[half, chunk_rows(me)], recv_ref.at[me, half], data_send.at[me, half, 0]
        )

    def stage(half, first_tile, count):
        lanes = slice(first_tile * LANES, (first_tile + count) * LANES)
        piece_groups = chunk_groups // pieces[half]
        together = min(16, piece_groups)
        unroll = min(8, piece_groups)

        def mix_piece(first_group):
            def some(i, c):
                total = jnp.zeros((8, count * LANES), F32)
                for j in range(0, together, 2):
                    total = total + mix(first_group + i * together + j, first_tile, count)
                acc[:, lanes] += total
                return c

            lax.fori_loop(0, piece_groups // together, some, 0)

        def one(step, carry):
            k = offset(step)
            dest = lax.rem(me + k, n)
            first_group = dest * chunk_groups
            if half == 0:
                if by_chunk:
                    for b in range(chunk // LANES):
                        coefficients(dest * chunk + b * LANES)
                load(dest, 1).wait()
                load(dest, 2).wait()
                for piece in range(pieces[0]):
                    piece_first = first_group + piece * piece_groups

                    def early(i, c, piece_first=piece_first):
                        build(piece_first + i)
                        products(piece_first + i, 1, tiles - 1)
                        return c

                    lax.fori_loop(0, piece_groups, early, 0, unroll=unroll)
                    if piece == 0:
                        load(dest, 0).wait()

                        @pl.when(step == 0)
                        def _():
                            pl.semaphore_wait(barrier, n - 1 + nz - 1)
                            make_masks()

                    if piece == pieces[0] - 1:
                        take_raw(dest)

                        @pl.when(me < n - 1)
                        def _():
                            raw_copy(dest).start()
                            product_copy(dest).start()

                    mix_piece(piece_first)

                    @pl.when(k != 0)
                    def _(piece=piece):
                        data_copy(dest, me, 0, piece).start()

            else:

                @pl.when(me > 0)
                def _():
                    raw_copy(dest).wait_recv()
                    product_copy(dest).wait_recv()

                spread_raw(dest)

                def rest(i, c):
                    products(first_group + i, 0, 1)
                    return c

                lax.fori_loop(0, chunk_groups, rest, 0, unroll=unroll)
                mix_piece(first_group)

                @pl.when(k != 0)
                def _():
                    data_copy(dest, me, 1, 0).start()

            @pl.when(k == 0)
            def _():
                own_copy(half).start()

            return carry

        lax.fori_loop(0, n, one, 0)

    stage(0, tiles // 2, tiles - tiles // 2)
    stage(1, 0, tiles // 2)

    sq_all[mz] = jnp.sum(acc[...], axis=0, keepdims=True)

    def sq_copy(dest, source):
        return pltpu.make_async_remote_copy(
            src_ref=sq_all.at[mz],
            dst_ref=sq_all.at[source],
            send_sem=sq_send.at[dest],
            recv_sem=sq_recv.at[source],
            device_id={"ch": dest},
        )

    for k in range(1, nz):
        sq_copy(lax.rem(mz + k, nz), mz).start()
    for k in range(1, nz):
        sq_copy(mz, lax.rem(mz + k, nz)).wait_recv()
    total = sq_all[0]
    for z in range(1, nz):
        total = total + sq_all[z]
    own_scale[0] = lax.rsqrt(total / D + NORM_EPS)
    keep_scale = pltpu.make_async_copy(own_scale.at[0], scale_ref.at[me], sc_send.at[me])
    keep_scale.start()

    def sc_copy(dest, source):
        return pltpu.make_async_remote_copy(
            src_ref=own_scale.at[0],
            dst_ref=scale_ref.at[source],
            send_sem=sc_send.at[dest],
            recv_sem=sc_recv.at[source],
            device_id={"ctx": dest},
        )

    for k in range(1, n):
        sc_copy(lax.rem(me + k, n), me).start()
    for k in range(1, n):
        sc_copy(me, lax.rem(me + k, n)).wait_recv()
    keep_scale.wait()

    def finish(k, carry):
        other = lax.rem(me + k, n)
        for half in (0, 1):
            for piece in range(pieces[half]):
                data_copy(me, other, half, piece).wait_recv()
                data_copy(other, me, half, piece).wait_send()
        sc_copy(other, me).wait_send()
        return carry

    lax.fori_loop(1, n, finish, 0)
    own_copy(0).wait()
    own_copy(1).wait()
    for k in range(1, nz):
        sq_copy(lax.rem(mz + k, nz), mz).wait_send()

    @pl.when(me < n - 1)
    def _():
        def sent(c, carry):
            raw_copy(c).wait_send()
            product_copy(c).wait_send()
            return carry

        lax.fori_loop(0, n, sent, 0)


def scale_kernel(source, scales_hbm, target, held, scaled, scales, scale_sem, load_sem, store_sem):
    n, _, _, width = source.shape
    fetch = pltpu.make_async_copy(scales_hbm, scales, scale_sem)
    fetch.start()
    loads, stores = [], []
    for i in range(n):
        lanes = slice(2 * i * width, 2 * (i + 1) * width)
        loads.append(pltpu.make_async_copy(source.at[i], held.at[i], load_sem.at[i]))
        stores.append(pltpu.make_async_copy(scaled.at[:, lanes], target.at[:, lanes], store_sem.at[i]))
        loads[i].start()
    fetch.wait()
    for i in range(n):
        loads[i].wait()
        for half in range(2):
            first = (2 * i + 1 - half) * width
            scale = scales[i, :, (1 - half) * width : (2 - half) * width]
            scaled[:, first : first + width] = (held[i, half].astype(F32) * scale).astype(BF16)
        stores[i].start()
    for store in stores:
        store.wait()


def local(
    n, nz, gate_input, key_input, value_input, short_filter, mr_filter, mr_skip, norm_gain, doc_lengths
):
    channels, rows_here = gate_input.shape
    chunk = channels // n
    groups = channels // GROUP
    tiles = rows_here // LANES
    ext = pltpu.VMEM((channels, rows_here + LANES), BF16)
    anywhere = pl.BlockSpec(memory_space=pl.ANY)
    hbm = pl.BlockSpec(memory_space=pltpu.HBM)
    dma = pltpu.SemaphoreType.DMA
    received, scales = pl.pallas_call(
        functools.partial(kernel, n, nz),
        out_shape=(
            jax.ShapeDtypeStruct((n, 2, chunk, rows_here // 2), BF16),
            jax.ShapeDtypeStruct((n, 1, rows_here), F32),
        ),
        in_specs=[hbm] * 7 + [pl.BlockSpec(memory_space=pltpu.SMEM)],
        out_specs=(anywhere, anywhere),
        scratch_shapes=[
            ext,
            ext,
            ext,
            ext,
            pltpu.VMEM((groups, LANES, LANES), BF16),
            pltpu.VMEM((channels, LANES), F32),
            pltpu.VMEM((tiles, 2 * LANES, LANES), BF16),
            pltpu.VMEM((8, rows_here), F32),
            pltpu.VMEM((2, channels, rows_here // 2), BF16),
            pltpu.VMEM((n, 16, chunk), BF16),
            pltpu.VMEM((n, 16, chunk), BF16),
            pltpu.VMEM((channels, LANES), BF16),
            pltpu.VMEM((channels, LANES), BF16),
            pltpu.VMEM((8, rows_here), F32),
            pltpu.VMEM((nz, 1, rows_here), F32),
            pltpu.VMEM((1, 1, rows_here), F32),
            pltpu.VMEM((3, SHORT, channels), F32),
            pltpu.VMEM((groups, MR), F32),
            pltpu.VMEM((1, channels), F32),
            pltpu.VMEM((1, channels), F32),
            dma((4,)),
            dma((n, 3)),
            dma((n, 2)),
            dma((n, 2)),
            dma((n, 2, 2)),
            dma((n, 2, 2)),
            dma((nz,)),
            dma((nz,)),
            dma((n,)),
            dma((n,)),
        ],
        compiler_params=pltpu.CompilerParams(
            collective_id=0, has_side_effects=True, vmem_limit_bytes=56 * 1024 * 1024
        ),
        cost_estimate=pl.CostEstimate(
            flops=channels * rows_here * 600, bytes_accessed=channels * rows_here * 8, transcendentals=0
        ),
    )(
        gate_input,
        key_input,
        value_input,
        short_filter,
        mr_filter,
        mr_skip.reshape(1, channels),
        norm_gain.reshape(1, channels),
        doc_lengths,
    )
    return pl.pallas_call(
        scale_kernel,
        out_shape=jax.ShapeDtypeStruct((chunk, n * rows_here), BF16),
        in_specs=[anywhere, anywhere],
        out_specs=anywhere,
        scratch_shapes=[
            pltpu.VMEM(received.shape, BF16),
            pltpu.VMEM((chunk, n * rows_here), BF16),
            pltpu.VMEM(scales.shape, F32),
            dma(()),
            dma((n,)),
            dma((n,)),
        ],
        compiler_params=pltpu.CompilerParams(vmem_limit_bytes=56 * 1024 * 1024),
    )(received, scales)


def solution(mesh):
    n, nz = mesh.shape["ctx"], mesh.shape["ch"]
    in_specs = (
        P("ch", "ctx"),
        P("ch", "ctx"),
        P("ch", "ctx"),
        P(None, None, "ch"),
        P("ch", None),
        P("ch"),
        P("ch"),
        P(),
    )
    out_specs = P(("ch", "ctx"), None)
    return jax.shard_map(
        functools.partial(local, n, nz), mesh=mesh, in_specs=in_specs, out_specs=out_specs, check_vma=False
    )
```

```python
import functools

import jax
import jax.numpy as jnp
from jax import lax
from jax.experimental import pallas as pl
from jax.experimental.pallas import tpu as pltpu
from jax.sharding import PartitionSpec as P

D = 8192
GROUP = 16
SHORT = 3
MR = 128
NORM_EPS = 1e-06

LANES = 128
F32 = jnp.float32
BF16 = jnp.bfloat16


def short_conv(ext_ref, coef_ref, rows, first_tile, tiles, which, m1, m2):
    width = (tiles + 1) * LANES
    x = ext_ref[rows, first_tile * LANES : first_tile * LANES + width].astype(F32)
    x1 = pltpu.roll(x, 1, 1)[:, LANES:]
    x2 = pltpu.roll(x, 2, 1)[:, LANES:]
    base = which * SHORT
    c0 = coef_ref[rows, base : base + 1]
    c1 = coef_ref[rows, base + 1 : base + 2]
    c2 = coef_ref[rows, base + 2 : base + 3]
    return c0 * x[:, LANES:] + c1 * (x1 * m1) + c2 * (x2 * m2)


def kernel(
    n,
    nz,
    gate_hbm,
    key_hbm,
    value_hbm,
    sf_hbm,
    mr_hbm,
    skip_hbm,
    gain_hbm,
    docs_ref,
    recv_ref,
    scale_ref,
    g_ext,
    k_ext,
    v_ext,
    p_ext,
    circ,
    coef,
    masks,
    lagmask,
    sendbuf,
    raw_send,
    raw_recv,
    halo_out,
    halo_in,
    acc,
    sq_all,
    own_scale,
    sf_ref,
    mr_ref,
    skip_ref,
    gain_ref,
    small_sem,
    load_sem,
    halo_send,
    halo_recv,
    data_send,
    data_recv,
    sq_send,
    sq_recv,
    sc_send,
    sc_recv,
):
    me = lax.axis_index("ctx")
    mz = lax.axis_index("ch")
    channels, rows_here = gate_hbm.shape
    chunk = channels // n
    groups = channels // GROUP
    tiles = rows_here // LANES
    chunk_groups = chunk // GROUP
    barrier = pltpu.get_barrier_semaphore()

    def offset(step):
        odd = (step + n // 2 + 1) // n
        return ((2 * (step + 1) + 3 * odd) % n) * (1 - (step + 1) // n)

    def load(b, which):
        source = (gate_hbm, key_hbm, value_hbm)[which]
        target = (g_ext, k_ext, v_ext)[which]
        span = pl.ds(pl.multiple_of(b * chunk, chunk), chunk)
        return pltpu.make_async_copy(
            source.at[span, :],
            target.at[span, LANES : LANES + rows_here],
            load_sem.at[b, which],
        )

    small = [
        pltpu.make_async_copy(source, target, small_sem.at[i])
        for i, (source, target) in enumerate(
            ((sf_hbm, sf_ref), (skip_hbm, skip_ref), (gain_hbm, gain_ref), (mr_hbm, mr_ref))
        )
    ]
    for copy in small:
        copy.start()
    for step in range(n):
        dest = lax.rem(me + offset(step), n)
        for which in (1, 2, 0):
            load(dest, which).start()
    for k in range(1, n):
        pl.semaphore_signal(barrier, inc=1, device_id={"ctx": lax.rem(me + k, n)})
    for k in range(1, nz):
        pl.semaphore_signal(barrier, inc=1, device_id={"ch": lax.rem(mz + k, nz)})

    positions = me * rows_here + lax.broadcasted_iota(jnp.int32, (1, rows_here), 1)
    starts = jnp.zeros((1, rows_here), jnp.int32)
    first = jnp.int32(0)
    for d in range(docs_ref.shape[0]):
        starts = jnp.where(positions >= first, first, starts)
        first = first + docs_ref[d]
    for lag in (1, 2):
        lagmask[lag : lag + 1, :] = jnp.where(positions - lag >= starts, 1.0, 0.0).astype(F32)
    for copy in small:
        copy.wait()

    def make_masks():
        s_index = lax.broadcasted_iota(jnp.int32, (LANES, LANES), 0)
        t_index = lax.broadcasted_iota(jnp.int32, (LANES, LANES), 1)
        for tile in range(tiles):
            start_row = starts[:, tile * LANES : (tile + 1) * LANES]
            here = me * rows_here + tile * LANES + s_index
            before = (t_index < s_index) & (here - LANES >= start_row)
            within = (t_index >= s_index) & (here >= start_row)
            masks[tile, 0:LANES, :] = jnp.where(before, 1.0, 0.0).astype(BF16)
            masks[tile, LANES : 2 * LANES, :] = jnp.where(within, 1.0, 0.0).astype(BF16)

    def coefficients(first):
        span = pl.ds(pl.multiple_of(first, LANES), LANES)
        parts = [sf_ref[a, :, span] for a in range(3)] + [skip_ref[:, span], gain_ref[:, span]]
        parts.append(jnp.zeros((5, LANES), F32))
        coef[span, 0:16] = jnp.concatenate(parts, axis=0).T

    by_chunk = chunk % LANES == 0
    if not by_chunk:
        for b in range(channels // LANES):
            coefficients(b * LANES)

    row16 = lax.broadcasted_iota(jnp.int32, (16, LANES), 0)
    lane16 = lax.broadcasted_iota(jnp.int32, (16, LANES), 1)

    def pick(which):
        hit = (lane16 - (LANES - 2) == row16 - 2 * which) & (lane16 >= LANES - 2)
        return jnp.where(hit, 1.0, 0.0).astype(BF16)

    last = tiles * LANES

    right = lax.rem(me + 1, n)

    def chunk_rows(c):
        return pl.ds(pl.multiple_of(c * chunk, chunk), chunk)

    def raw_copy(c):
        return pltpu.make_async_remote_copy(
            src_ref=raw_send.at[c],
            dst_ref=raw_recv.at[c],
            send_sem=halo_send.at[c, 0],
            recv_sem=halo_recv.at[c, 0],
            device_id={"ctx": right},
        )

    def product_copy(c):
        return pltpu.make_async_remote_copy(
            src_ref=halo_out.at[chunk_rows(c)],
            dst_ref=halo_in.at[chunk_rows(c)],
            send_sem=halo_send.at[c, 1],
            recv_sem=halo_recv.at[c, 1],
            device_id={"ctx": right},
        )

    @pl.when(me == 0)
    def _():
        raw_recv[...] = jnp.zeros(raw_recv.shape, BF16)
        halo_in[...] = jnp.zeros(halo_in.shape, BF16)

    def take_raw(c):
        columns = jnp.zeros((16, chunk), F32)
        for which, ref in enumerate((g_ext, k_ext, v_ext)):
            columns = columns + lax.dot_general(
                pick(which),
                ref[chunk_rows(c), last : last + LANES],
                (((1,), (1,)), ((), ())),
                preferred_element_type=F32,
            )
        raw_send[c] = columns.astype(BF16)

    def spread_raw(c):
        for which, ref in enumerate((g_ext, k_ext, v_ext)):
            ref[chunk_rows(c), 0:LANES] = lax.dot_general(
                raw_recv[c],
                pick(which),
                (((0,), (0,)), ((), ())),
                preferred_element_type=F32,
            ).astype(BF16)

    def build(g):
        taps = jnp.broadcast_to(mr_ref[pl.ds(g, 1), :], (LANES, LANES))
        circ[g] = pltpu.roll(taps, 0, 1, stride=1, stride_axis=0).astype(BF16)

    def products(g, first_tile, count):
        rows = pl.ds(pl.multiple_of(g * GROUP, GROUP), GROUP)
        lanes = slice(first_tile * LANES, (first_tile + count) * LANES)
        m1, m2 = lagmask[1:2, lanes], lagmask[2:3, lanes]
        kc = short_conv(k_ext, coef, rows, first_tile, count, 1, m1, m2)
        vc = short_conv(v_ext, coef, rows, first_tile, count, 2, m1, m2)
        result = (kc * vc).astype(BF16)
        p_ext[rows, (first_tile + 1) * LANES : (first_tile + 1 + count) * LANES] = result
        if first_tile + count == tiles:
            halo_out[rows] = result[:, (count - 1) * LANES :]

    acc[...] = jnp.zeros(acc.shape, F32)

    def mix(g, first_tile, count):
        rows = pl.ds(pl.multiple_of(g * GROUP, 2 * GROUP), 2 * GROUP)
        lanes = slice(first_tile * LANES, (first_tile + count) * LANES)
        both = jnp.concatenate([circ[g], circ[g + 1]], axis=1)
        pair = jnp.concatenate([both, both], axis=0)
        parts = []
        for tile in range(first_tile, first_tile + count):
            mask = masks[tile]
            if tile == 0:
                window = jnp.concatenate([halo_in[rows], p_ext[rows, LANES : 2 * LANES]], axis=1)
            else:
                window = p_ext[rows, tile * LANES : (tile + 2) * LANES]
            result = jnp.dot(
                window,
                pair * jnp.concatenate([mask, mask], axis=1),
                preferred_element_type=F32,
            )
            parts.append(
                jnp.concatenate([result[:GROUP, :LANES], result[GROUP:, LANES:]], axis=0)
            )
        mixed = parts[0] if count == 1 else jnp.concatenate(parts, axis=1)
        direct = p_ext[rows, (first_tile + 1) * LANES : (first_tile + 1 + count) * LANES]
        mixed = mixed + coef[rows, 9:10] * direct.astype(F32)
        gate = short_conv(
            g_ext, coef, rows, first_tile, count, 0, lagmask[1:2, lanes], lagmask[2:3, lanes]
        )
        gated = gate * mixed
        sendbuf[0 if first_tile else 1, rows] = (gated * coef[rows, 10:11]).astype(BF16)
        squares = gated * gated
        return squares[0:8] + squares[8:16] + squares[16:24] + squares[24:32]

    def data_copy(dest, source, half):
        return pltpu.make_async_remote_copy(
            src_ref=sendbuf.at[half, chunk_rows(dest)],
            dst_ref=recv_ref.at[source, half],
            send_sem=data_send.at[dest, half],
            recv_sem=data_recv.at[source, half],
            device_id={"ctx": dest},
        )

    def own_copy(half):
        return pltpu.make_async_copy(
            sendbuf.at[half, chunk_rows(me)], recv_ref.at[me, half], data_send.at[me, half]
        )

    def stage(half, first_tile, count):
        lanes = slice(first_tile * LANES, (first_tile + count) * LANES)
        together = min(16, chunk_groups)
        unroll = min(16, chunk_groups)

        def one(step, carry):
            k = offset(step)
            dest = lax.rem(me + k, n)
            first_group = dest * chunk_groups
            if half == 0:
                if by_chunk:
                    for b in range(chunk // LANES):
                        coefficients(dest * chunk + b * LANES)
                load(dest, 1).wait()
                load(dest, 2).wait()

                def early(i, c):
                    build(first_group + i)
                    products(first_group + i, 1, tiles - 1)
                    return c

                lax.fori_loop(0, chunk_groups, early, 0, unroll=unroll)
                load(dest, 0).wait()
                take_raw(dest)

                @pl.when(step == 0)
                def _():
                    pl.semaphore_wait(barrier, n - 1 + nz - 1)

                @pl.when(me < n - 1)
                def _():
                    raw_copy(dest).start()
                    product_copy(dest).start()

                @pl.when(step == 0)
                def _():
                    make_masks()

            else:

                @pl.when(me > 0)
                def _():
                    raw_copy(dest).wait_recv()
                    product_copy(dest).wait_recv()

                spread_raw(dest)

                def rest(i, c):
                    products(first_group + i, 0, 1)
                    return c

                lax.fori_loop(0, chunk_groups, rest, 0, unroll=unroll)

            def some(i, c):
                total = jnp.zeros((8, count * LANES), F32)
                for j in range(0, together, 2):
                    total = total + mix(first_group + i * together + j, first_tile, count)
                acc[:, lanes] += total
                return c

            lax.fori_loop(0, chunk_groups // together, some, 0)

            @pl.when(k != 0)
            def _():
                data_copy(dest, me, half).start()

            @pl.when(k == 0)
            def _():
                own_copy(half).start()

            return carry

        lax.fori_loop(0, n, one, 0)

    stage(0, tiles // 2, tiles - tiles // 2)
    stage(1, 0, tiles // 2)

    sq_all[mz] = jnp.sum(acc[...], axis=0, keepdims=True)

    def sq_copy(dest, source):
        return pltpu.make_async_remote_copy(
            src_ref=sq_all.at[mz],
            dst_ref=sq_all.at[source],
            send_sem=sq_send.at[dest],
            recv_sem=sq_recv.at[source],
            device_id={"ch": dest},
        )

    for k in range(1, nz):
        sq_copy(lax.rem(mz + k, nz), mz).start()
    for k in range(1, nz):
        sq_copy(mz, lax.rem(mz + k, nz)).wait_recv()
    total = sq_all[0]
    for z in range(1, nz):
        total = total + sq_all[z]
    own_scale[0] = lax.rsqrt(total / D + NORM_EPS)
    keep_scale = pltpu.make_async_copy(own_scale.at[0], scale_ref.at[me], sc_send.at[me])
    keep_scale.start()

    def sc_copy(dest, source):
        return pltpu.make_async_remote_copy(
            src_ref=own_scale.at[0],
            dst_ref=scale_ref.at[source],
            send_sem=sc_send.at[dest],
            recv_sem=sc_recv.at[source],
            device_id={"ctx": dest},
        )

    for k in range(1, n):
        sc_copy(lax.rem(me + k, n), me).start()
    for k in range(1, n):
        sc_copy(me, lax.rem(me + k, n)).wait_recv()
    keep_scale.wait()

    def finish(k, carry):
        other = lax.rem(me + k, n)
        for half in (0, 1):
            data_copy(me, other, half).wait_recv()
            data_copy(other, me, half).wait_send()
        sc_copy(other, me).wait_send()
        return carry

    lax.fori_loop(1, n, finish, 0)
    own_copy(0).wait()
    own_copy(1).wait()
    for k in range(1, nz):
        sq_copy(lax.rem(mz + k, nz), mz).wait_send()

    @pl.when(me < n - 1)
    def _():
        def sent(c, carry):
            raw_copy(c).wait_send()
            product_copy(c).wait_send()
            return carry

        lax.fori_loop(0, n, sent, 0)


def scale_kernel(source, scales_hbm, target, held, scaled, scales, scale_sem, load_sem, store_sem):
    n, _, _, width = source.shape
    fetch = pltpu.make_async_copy(scales_hbm, scales, scale_sem)
    fetch.start()
    loads, stores = [], []
    for i in range(n):
        lanes = slice(2 * i * width, 2 * (i + 1) * width)
        loads.append(pltpu.make_async_copy(source.at[i], held.at[i], load_sem.at[i]))
        stores.append(pltpu.make_async_copy(scaled.at[:, lanes], target.at[:, lanes], store_sem.at[i]))
        loads[i].start()
    fetch.wait()
    for i in range(n):
        loads[i].wait()
        for half in range(2):
            first = (2 * i + 1 - half) * width
            scale = scales[i, :, (1 - half) * width : (2 - half) * width]
            scaled[:, first : first + width] = (held[i, half].astype(F32) * scale).astype(BF16)
        stores[i].start()
    for store in stores:
        store.wait()


def local(
    n, nz, gate_input, key_input, value_input, short_filter, mr_filter, mr_skip, norm_gain, doc_lengths
):
    channels, rows_here = gate_input.shape
    chunk = channels // n
    groups = channels // GROUP
    tiles = rows_here // LANES
    ext = pltpu.VMEM((channels, rows_here + LANES), BF16)
    anywhere = pl.BlockSpec(memory_space=pl.ANY)
    hbm = pl.BlockSpec(memory_space=pltpu.HBM)
    dma = pltpu.SemaphoreType.DMA
    received, scales = pl.pallas_call(
        functools.partial(kernel, n, nz),
        out_shape=(
            jax.ShapeDtypeStruct((n, 2, chunk, rows_here // 2), BF16),
            jax.ShapeDtypeStruct((n, 1, rows_here), F32),
        ),
        in_specs=[hbm] * 7 + [pl.BlockSpec(memory_space=pltpu.SMEM)],
        out_specs=(anywhere, anywhere),
        scratch_shapes=[
            ext,
            ext,
            ext,
            ext,
            pltpu.VMEM((groups, LANES, LANES), BF16),
            pltpu.VMEM((channels, LANES), F32),
            pltpu.VMEM((tiles, 2 * LANES, LANES), BF16),
            pltpu.VMEM((8, rows_here), F32),
            pltpu.VMEM((2, channels, rows_here // 2), BF16),
            pltpu.VMEM((n, 16, chunk), BF16),
            pltpu.VMEM((n, 16, chunk), BF16),
            pltpu.VMEM((channels, LANES), BF16),
            pltpu.VMEM((channels, LANES), BF16),
            pltpu.VMEM((8, rows_here), F32),
            pltpu.VMEM((nz, 1, rows_here), F32),
            pltpu.VMEM((1, 1, rows_here), F32),
            pltpu.VMEM((3, SHORT, channels), F32),
            pltpu.VMEM((groups, MR), F32),
            pltpu.VMEM((1, channels), F32),
            pltpu.VMEM((1, channels), F32),
            dma((4,)),
            dma((n, 3)),
            dma((n, 2)),
            dma((n, 2)),
            dma((n, 2)),
            dma((n, 2)),
            dma((nz,)),
            dma((nz,)),
            dma((n,)),
            dma((n,)),
        ],
        compiler_params=pltpu.CompilerParams(
            collective_id=0, has_side_effects=True, vmem_limit_bytes=56 * 1024 * 1024
        ),
        cost_estimate=pl.CostEstimate(
            flops=channels * rows_here * 600, bytes_accessed=channels * rows_here * 8, transcendentals=0
        ),
    )(
        gate_input,
        key_input,
        value_input,
        short_filter,
        mr_filter,
        mr_skip.reshape(1, channels),
        norm_gain.reshape(1, channels),
        doc_lengths,
    )
    return pl.pallas_call(
        scale_kernel,
        out_shape=jax.ShapeDtypeStruct((chunk, n * rows_here), BF16),
        in_specs=[anywhere, anywhere],
        out_specs=anywhere,
        scratch_shapes=[
            pltpu.VMEM(received.shape, BF16),
            pltpu.VMEM((chunk, n * rows_here), BF16),
            pltpu.VMEM(scales.shape, F32),
            dma(()),
            dma((n,)),
            dma((n,)),
        ],
        compiler_params=pltpu.CompilerParams(vmem_limit_bytes=56 * 1024 * 1024),
    )(received, scales)


def solution(mesh):
    n, nz = mesh.shape["ctx"], mesh.shape["ch"]
    in_specs = (
        P("ch", "ctx"),
        P("ch", "ctx"),
        P("ch", "ctx"),
        P(None, None, "ch"),
        P("ch", None),
        P("ch"),
        P("ch"),
        P(),
    )
    out_specs = P(("ch", "ctx"), None)
    return jax.shard_map(
        functools.partial(local, n, nz), mesh=mesh, in_specs=in_specs, out_specs=out_specs, check_vma=False
    )
```
